256 devices in a mesh: blk: 16 (over y_lo, x, core), grp: 16 (over z, y_hi).
Axes of the slice: x: 4, y: 4 (y_hi: 2, y_lo: 2; y = y_hi * 2 + y_lo), z: 8, core: 2. Of those that a mesh axis runs over, the one named last changes fastest.
Arguments:
- user_factors: bfloat16 [16, 32768, 256], P('grp', 'blk')
- item_factors: bfloat16 [2048, 256], P('blk'), may hold values from -1.5 to 1.5
- tile_user: int32 [16, 16, 8], P('blk', 'grp'), may hold values from 0 to 255, as said below
- tile_weight: bfloat16 [16, 16, 8, 128, 128], P('blk', 'grp'), may hold values from 0.024 to 40.5
- tile_target: bfloat16 [16, 16, 8, 128, 128], P('blk', 'grp'), may hold values from -16 to 16
Outputs:
- new_block: float32 [2048, 128], P(('blk', 'grp'))
The draws below stay inside these ranges and needn't reach their ends.
Inputs may be any that keep to these rules, and one draw needn't show every extreme that they name: `tile_user`: for each item block and user group, 8 different user tiles in increasing order.
All inputs are finite; a program needn't handle non-finite values.
Results may differ from the reference program's by a relative error of at most 0.002.
The reference program's roundings to bfloat16 on the way count: a program that leaves them out, or rounds other values in their place, can miss the bound.
Values may be sent and summed in bfloat16 or wider, within the bound.
A program may use at most 128 MiB of HBM per device.

```python
import math
import jax
import jax.numpy as jnp
from jax import lax

K = 256
KB = 128
TILE = 128
NT = 8
UT_DEV = 16
GUSERS = 32768
ITEMS = 2048
N_BLK = 16
N_GRP = 16


def rotate_columns(values, key):
    column_count = values.shape[-1]
    leading = values.shape[:-1]
    section_count = column_count.bit_length() - 1
    for section_index in range(section_count):
        stride = 1 << section_index
        pair_count = column_count // (2 * stride)
        shaped = values.reshape(leading + (pair_count, 2, stride))
        first_half = shaped[..., 0, :]
        second = shaped[..., 1, :]
        angle_draw = jax.random.uniform(jax.random.fold_in(key, section_index), (pair_count, stride), jnp.float32, -math.pi, math.pi)
        cosine = jnp.cos(angle_draw)
        sine_part = jnp.sin(angle_draw)
        turned_first = first_half * cosine - second * sine_part
        turned_second = first_half * sine_part + second * cosine
        values = jnp.stack([turned_first, turned_second], axis=-2).reshape(leading + (column_count,))
    return values


def draw_user_factors(key, part):
    key = jax.random.fold_in(key, 1)
    base_key, row_key, spectrum_key, tile_key, turn_key = jax.random.split(key, 5)
    base_values = jax.random.normal(base_key, (N_GRP, GUSERS, K), jnp.float32)
    spectrum = jnp.exp(jax.random.uniform(spectrum_key, (K,), jnp.float32, 0.0, 2.4849066))
    tile_spread = jnp.exp(jax.random.uniform(tile_key, (N_GRP, GUSERS // TILE, 1, K), jnp.float32, -1.0986123, 1.0986123))
    shaped = base_values.reshape(N_GRP, GUSERS // TILE, TILE, K) * tile_spread * spectrum * (1.0 / 7.7)
    mixed = rotate_columns(shaped.reshape(N_GRP, GUSERS, K), turn_key)
    row_place = (jnp.arange(N_GRP)[:, None] * GUSERS + jnp.arange(GUSERS)[None, :]).astype(jnp.float32) / (N_GRP * GUSERS)
    rising = 0.6 + 1.2 * row_place
    row_scale = jnp.exp(jax.random.uniform(row_key, (N_GRP, GUSERS), jnp.float32, -0.6931472, 0.6931472))
    return (mixed * 0.25 * (rising * row_scale)[:, :, None]).astype(jnp.bfloat16)


def draw_tile_user(key, part):
    key = jax.random.fold_in(key, 2)
    score_key, hot_key = jax.random.split(key)
    entry_count = UT_DEV * N_BLK
    rating_scores = jax.random.randint(score_key, (N_BLK, N_GRP, entry_count), 0, 1 << 16)
    popular_items = jax.random.randint(hot_key, (N_BLK, N_GRP, N_BLK), 0, 3)
    popular_items = jnp.repeat(popular_items, UT_DEV, axis=2)
    item_indices = jnp.arange(entry_count)
    block_ends = ((item_indices == 0) | (item_indices == entry_count - 1)).astype(jnp.int32)
    leading_index = ((jnp.arange(N_BLK)[:, None] == 0) & (jnp.arange(N_GRP)[None, :] == 0)).astype(jnp.int32)
    extra_weight = leading_index[:, :, None] * block_ends[None, None, :] * 4
    grand_total = ((rating_scores + (popular_items + extra_weight) * (1 << 16)) * entry_count + item_indices[None, None, :]).astype(jnp.int32)
    picked = jax.lax.top_k(grand_total, NT)[1]
    return jnp.sort(picked, axis=-1).astype(jnp.int32)


def draw_tile_weight(key, part):
    key = jax.random.fold_in(key, 3)
    item_key, entry_key = jax.random.split(key)
    item_level = jax.random.uniform(item_key, (N_BLK, N_GRP, NT, 1, TILE), jnp.float32, 0.0, 1.0)
    item_scale = 0.05 * jnp.exp(5.9914645 * item_level)
    entry_scale = jnp.exp(jax.random.uniform(entry_key, (N_BLK, N_GRP, NT, TILE, TILE), jnp.float32, -0.6931472, 0.6931472))
    return (item_scale * entry_scale).astype(jnp.bfloat16)


def block_levels(stream_key, shape, shards, least, top_value):
    def one(position, blocks):
        steps = jax.random.uniform(jax.random.fold_in(jax.random.fold_in(stream_key, 6), position), (blocks,), jnp.float32, least / len(shards), top_value / len(shards))
        return jnp.repeat(jnp.exp(steps), shape[position] // blocks).reshape((-1,) + (1,) * (len(shape) - position - 1))

    factor_of = one(*shards[0])
    for cut in shards[1:]:
        factor_of = factor_of * one(*cut)
    return factor_of


def normal_values(stream_key, dims, deviation, limit, pieces=(), dtype=jnp.bfloat16):
    factor_of = block_levels(stream_key, dims, pieces, -0.22, 0.18) if pieces else 1.0
    drawn = jax.random.normal(stream_key, dims, jnp.float32) * deviation * factor_of
    return jnp.minimum(jnp.maximum(drawn, -limit), limit).astype(dtype)


def setup_inputs(seed: int = 0) -> dict:
    arg_keys = jax.random.split(jax.random.key(seed), 6)
    return {
        "user_factors": draw_user_factors(jax.random.fold_in(arg_keys[5], 71), 0),
        "item_factors": normal_values(arg_keys[1], (ITEMS, K), 0.25, 1.5, ((0, 16),)),
        "tile_user": draw_tile_user(jax.random.fold_in(arg_keys[5], 71), 0),
        "tile_weight": draw_tile_weight(jax.random.fold_in(arg_keys[5], 71), 0),
        "tile_target": normal_values(arg_keys[4], (N_BLK, N_GRP, NT, TILE, TILE), 4.0, 16.0, ((0, 16), (1, 16))),
    }


prior_weight = 0.05
item_group = 8

def reference(user_factors, item_factors, tile_user, tile_weight, tile_target):
    w_all = user_factors.reshape(-1, K)
    gram = jnp.dot(w_all[:, :KB].T.astype(jnp.float32), w_all.astype(jnp.float32), preferred_element_type=jnp.float32)
    items = item_factors.reshape(N_BLK, TILE, K)
    offsets = jnp.arange(TILE).astype(jnp.int32)

    def one_block(args):
        h_blk, users_idx, weight, target = args
        rows_idx = (users_idx[..., None] * TILE + offsets).astype(jnp.int32)
        rows = jax.vmap(lambda w_grp, r_grp: w_grp[r_grp])(user_factors, rows_idx)
        rows_flat = rows.reshape(-1, K)
        w_block = rows_flat[:, :KB]
        pred = jnp.dot(rows_flat.astype(jnp.float32), h_blk.T.astype(jnp.float32), preferred_element_type=jnp.float32)
        w_flat = weight.reshape(-1, TILE)
        t_flat = target.reshape(-1, TILE)
        resid = (w_flat.astype(jnp.float32) * (pred - t_flat.astype(jnp.float32))).astype(jnp.bfloat16)
        grad = jnp.dot(resid.T.astype(jnp.float32), w_block.astype(jnp.float32), preferred_element_type=jnp.float32)
        grad = grad + prior_weight * jnp.dot(h_blk.astype(jnp.float32), gram.T, precision=lax.Precision.HIGHEST)

        def sub(j):
            cols = lax.dynamic_slice_in_dim(w_flat, (j * item_group).astype(jnp.int32), item_group, 1)
            weighted = (cols.astype(jnp.float32)[:, :, None] * w_block.astype(jnp.float32)[:, None, :]).astype(jnp.bfloat16)
            weighted = weighted.reshape(-1, item_group * KB)
            return jnp.dot(weighted.T.astype(jnp.float32), w_block.astype(jnp.float32), preferred_element_type=jnp.float32).reshape(item_group, KB, KB)
        hess = lax.map(sub, jnp.arange(TILE // item_group).astype(jnp.int32)).reshape(TILE, KB, KB)
        hess = hess + prior_weight * gram[:, :KB][None]
        factor = jnp.linalg.cholesky(hess)
        delta = jax.scipy.linalg.cho_solve((factor, True), grad[..., None])[..., 0]
        return h_blk[:, :KB].astype(jnp.float32) - delta
    result = lax.map(one_block, (items, tile_user, tile_weight, tile_target))
    return result.reshape(ITEMS, KB)
```

```python
import functools

import jax
import jax.numpy as jnp
from jax import lax
from jax.experimental import pallas as pl
from jax.experimental.pallas import tpu as pltpu
from jax.sharding import PartitionSpec as P

F32 = jnp.float32
BF16 = jnp.bfloat16
MESH = pl.DeviceIdType.MESH
K = 256
KB = 128
TILE = 128
NT = 8
PRIOR = 0.05
NI = 8
OWN = 16
ROWS = 64
NQ = TILE // ROWS
NCH = 2 * NQ
CU = NT * ROWS
NZ = 8
BOTH_LAST = (((1,), (1,)), ((), ()))
BOTH_FIRST = (((0,), (0,)), ((), ()))


def gather_kernel(
    user_ref, tile_ref, item_ref, weight_ref, target_ref,
    hess_ref, grad_ref, gram_ref,
    pools, far_a, far_b, out_p, out_m, in_a, in_b, in_p, in_m, rights, zbufs,
    reqs, item, weight, target, wt_own, tt_own, wz, hacc, hin, gsend, gin,
    gpart, gin1, gone, gin2, gtwo, gall, local_sem, send_sem, recv_sem,
):
    me_b, me_g = lax.axis_index("blk"), lax.axis_index("grp")
    y_lo, x, core = me_b // 8, lax.rem(me_b // 2, 4), lax.rem(me_b, 2)
    z, y_hi = me_g // 2, lax.rem(me_g, 2)
    own = y_lo * 2 + core
    across = (1 - y_lo) * 2 + core
    sibling = (me_b + 1 - 2 * core, me_g)
    y_peer = (lax.rem(me_b + 8, 16), me_g)
    x_at = [lax.rem(x + k, 4) for k in range(4)]
    x_peer = [(y_lo * 8 + x_at[k] * 2 + core, me_g) for k in range(4)]
    z_at = [lax.rem(z + k, NZ) for k in range(NZ)]
    z_peer = [(me_b, z_at[k] * 2 + y_hi) for k in range(NZ)]
    blk_at = [lax.rem(me_b + k, 16) for k in range(16)]
    grp_at = [lax.rem(me_g + k, 16) for k in range(16)]
    blk_peer = [(blk_at[k], me_g) for k in range(16)]
    grp_peer = [(me_b, grp_at[k]) for k in range(16)]
    partner = (me_b, me_g + 1 - 2 * y_hi)

    slots, sent = {}, []

    def slot(name):
        return slots.setdefault(name, len(slots))

    def send(name, src, dst, device):
        k = slot(name)
        copy = pltpu.make_async_remote_copy(
            src_ref=src, dst_ref=dst, send_sem=send_sem.at[k], recv_sem=recv_sem.at[k],
            device_id=device, device_id_type=MESH)
        copy.start()
        sent.append(copy)

    def arrived(name, dst):
        k = slot(name)
        pltpu.make_async_remote_copy(
            src_ref=dst, dst_ref=dst, send_sem=send_sem.at[k], recv_sem=recv_sem.at[k],
            device_id=sibling, device_id_type=MESH).wait_recv()

    locals_ = {}

    def fetch(name, src, dst):
        copy = pltpu.make_async_copy(src, dst, local_sem.at[len(locals_)])
        copy.start()
        locals_[name] = copy

    for c in range(NCH):
        rows, cols = (c % NQ) * ROWS, (c // NQ) * KB
        fetch(("pool", c), user_ref.at[:, pl.ds(rows, ROWS), pl.ds(cols, KB)], pools[c].at[own])
    fetch("tile", tile_ref, reqs.at[x])
    fetch("weight", weight_ref, weight)
    fetch("target", target_ref, target)
    fetch("item", item_ref, item)

    barrier = pltpu.get_barrier_semaphore()
    for k in range(1, 16):
        pl.semaphore_signal(barrier, inc=1, device_id=blk_peer[k], device_id_type=MESH)
        pl.semaphore_signal(barrier, inc=1, device_id=grp_peer[k], device_id_type=MESH)
    for copy in locals_.values():
        copy.wait()
    pl.semaphore_wait(barrier, 30)

    def send_chunk(c):
        send(("y", c), pools[c].at[own], pools[c].at[own], y_peer)
        send(("s", c), pools[c].at[own], pools[c].at[own], sibling)

    def forward_chunk(c):
        arrived(("y", c), pools[c].at[across])
        send(("f", c), pools[c].at[across], pools[c].at[across], sibling)

    def finish_pool(c):
        other = y_lo * 2 + 1 - core
        diagonal = (1 - y_lo) * 2 + 1 - core
        arrived(("s", c), pools[c].at[other])
        arrived(("f", c), pools[c].at[diagonal])

    def wanted(k, j):
        return reqs[x_at[k], 0, j]

    def column(t):
        return jnp.bitwise_and(jnp.right_shift(t, 5), 3)

    def pick(c, t):
        owner = jnp.right_shift(t, 7) * 2 + jnp.bitwise_and(jnp.right_shift(t, 4), 1)
        return pools[c][owner, jnp.bitwise_and(t, 15)]

    half = ROWS // 2

    def x_pack(c):
        for j in range(NT):
            v = pick(c, wanted(2, j))
            far_a[c][j] = v[:half]
            far_b[c][j] = v[half:]
        send(("xa", c), far_a[c], in_a[c], x_peer[1])
        send(("xb", c), far_b[c], in_b[c], x_peer[3])
        for j in range(NT):
            out_p[c][1, j] = pick(c, wanted(1, j))[half:]
            out_m[c][0, j] = pick(c, wanted(3, j))[:half]
        send(("p1", c), out_p[c].at[1], in_m[c].at[1], x_peer[1])
        send(("m0", c), out_m[c].at[0], in_p[c].at[0], x_peer[3])

    def x_merge(c):
        arrived(("xa", c), in_a[c])
        for j in range(NT):
            t = wanted(1, j)
            out_p[c][0, j] = jnp.where(column(t) == x, pick(c, t)[:half], in_a[c][j])
        send(("p0", c), out_p[c].at[0], in_m[c].at[0], x_peer[1])
        arrived(("xb", c), in_b[c])
        for j in range(NT):
            t = wanted(3, j)
            out_m[c][1, j] = jnp.where(column(t) == x, pick(c, t)[half:], in_b[c][j])
        send(("m1", c), out_m[c].at[1], in_p[c].at[1], x_peer[3])

    def x_final(c):
        arrived(("p1", c), in_m[c].at[1])
        arrived(("m0", c), in_p[c].at[0])
        arrived(("p0", c), in_m[c].at[0])
        arrived(("m1", c), in_p[c].at[1])
        for j in range(NT):
            t = wanted(0, j)
            away = jnp.bitwise_and(column(t) - x + 4, 3)
            mine = pick(c, t)
            first = jnp.where(away == 0, mine[:half], jnp.where(away == 1, in_p[c][0, j], in_m[c][0, j]))
            second = jnp.where(away == 0, mine[half:], jnp.where(away == 3, in_m[c][1, j], in_p[c][1, j]))
            if c < NQ:
                zbufs[c][z, j, :half] = first
                zbufs[c][z, j, half:] = second
            else:
                rights[c - NQ][j, :half] = first
                rights[c - NQ][j, half:] = second

    def z_start(q):
        send(("zr", q, 1), zbufs[q].at[z], zbufs[q].at[z], z_peer[1])
        send(("zl", q, 1), zbufs[q].at[z], zbufs[q].at[z], z_peer[7])

    def z_hop(q, h):
        if h < 4:
            from_left, from_right = z_at[NZ - h], z_at[h]
            arrived(("zr", q, h), zbufs[q].at[from_left])
            part = zbufs[q].at[from_left] if h < 3 else zbufs[q].at[from_left, pl.ds(0, NT // 2)]
            send(("zr", q, h + 1), part, part, z_peer[1])
            arrived(("zl", q, h), zbufs[q].at[from_right])
            part = zbufs[q].at[from_right] if h < 3 else zbufs[q].at[from_right, pl.ds(NT // 2, NT // 2)]
            send(("zl", q, h + 1), part, part, z_peer[7])
        else:
            arrived(("zr", q, 4), zbufs[q].at[z_at[4], pl.ds(0, NT // 2)])
            arrived(("zl", q, 4), zbufs[q].at[z_at[4], pl.ds(NT // 2, NT // 2)])

    def transposed(ref, out):
        span = TILE // ROWS
        for q in range(NQ):
            for p in range(NT // span):
                block = ref[p * span:(p + 1) * span, q * ROWS:(q + 1) * ROWS, :].reshape(TILE, TILE)
                out[:, :, pl.ds((q * (NT // span) + p) * TILE, TILE)] = block.T.reshape(NZ, 16, TILE)

    def send_weights():
        transposed(weight, wt_own)
        for k in range(1, NZ):
            send(("w", k), wt_own.at[z_at[k]], wz.at[z], z_peer[k])
        wz[z] = wt_own[z]

    def weights_arrived():
        for k in range(1, NZ):
            arrived(("w", k), wz.at[z_at[NZ - k]])

    def gram_start():
        left = jnp.zeros((KB, KB), F32)
        right = jnp.zeros((KB, KB), F32)
        for q in range(NQ):
            a = pools[q][own].reshape(OWN * ROWS, KB)
            b = pools[NQ + q][own].reshape(OWN * ROWS, KB)
            left += lax.dot_general(a, a, BOTH_FIRST, preferred_element_type=F32)
            right += lax.dot_general(a, b, BOTH_FIRST, preferred_element_type=F32)
        gpart[:, 0] = left.reshape(16, 8, KB)
        gpart[:, 1] = right.reshape(16, 8, KB)
        for k in range(1, 16):
            send(("g1", k), gpart.at[blk_at[k]], gin1.at[me_b], blk_peer[k])
        gin1[me_b] = gpart[me_b]

    def gram_second():
        for k in range(1, 16):
            arrived(("g1", k), gin1.at[blk_at[16 - k]])
        gone[...] = jnp.sum(gin1[...], axis=0)
        for k in range(1, 16):
            send(("g2", k), gone, gin2.at[me_g], grp_peer[k])
        gin2[me_g] = gone[...]

    def gram_third():
        for k in range(1, 16):
            arrived(("g2", k), gin2.at[grp_at[16 - k]])
        gtwo[...] = jnp.sum(gin2[...], axis=0)
        for k in range(1, 16):
            send(("g3", k), gtwo, gall.at[me_b], blk_peer[k])
        gall[me_b] = gtwo[...]

    def gram_last():
        for k in range(1, 16):
            arrived(("g3", k), gall.at[blk_at[16 - k]])
        gram_ref[...] = gall[...]

    GROUP = 4

    def hess_piece(q, source, first=0, count=16, start=False):
        users = zbufs[q][source].reshape(CU, KB)
        users_t = jnp.concatenate(
            [users[p * KB:(p + 1) * KB].T for p in range(CU // KB)], axis=1)
        users_t = users_t.reshape(KB // 16, 16, CU)
        scale = wz[source, :, pl.ds(q * CU, CU)].astype(F32)
        for i0 in range(0, 16, GROUP):
            lhs = []
            for i in range(i0, i0 + GROUP):
                row = jnp.broadcast_to(scale[i:i + 1], (16, CU)).astype(BF16)
                lhs.append((row[None] * users_t).reshape(KB, CU))
            part = jnp.dot(jnp.concatenate(lhs, axis=0), users, preferred_element_type=F32)
            part = part.reshape(GROUP, KB, KB)
            if start:
                hacc[i0:i0 + GROUP] = part
            else:
                hacc[i0:i0 + GROUP] += part

    def grad_start():
        total = jnp.zeros((TILE, KB), F32)
        items = item[...]
        for q in range(NQ):
            left = zbufs[q][z].reshape(CU, KB)
            right = rights[q][...].reshape(CU, KB)
            pred = lax.dot_general(items[:, :KB], left, BOTH_LAST, preferred_element_type=F32)
            pred += lax.dot_general(items[:, KB:], right, BOTH_LAST, preferred_element_type=F32)
            w = wt_own[:, :, pl.ds(q * CU, CU)].reshape(TILE, CU).astype(F32)
            t = tt_own[:, :, pl.ds(q * CU, CU)].reshape(TILE, CU).astype(F32)
            resid = (w * (pred - t)).astype(BF16)
            total += jnp.dot(resid, left, preferred_element_type=F32)
        gsend[...] = total.reshape(16, NI, KB)
        for k in range(1, 16):
            send(("gr", k), gsend.at[grp_at[k]], gin.at[me_g], grp_peer[k])
        gin[me_g] = gsend[me_g]

    def grad_last():
        for k in range(1, 16):
            arrived(("gr", k), gin.at[grp_at[16 - k]])
        grad_ref[...] = jnp.sum(gin[...], axis=0)

    def send_requests():
        for k in range(1, 4):
            send(("rq", k), reqs.at[x], reqs.at[x], x_peer[k])

    def requests_arrived():
        for k in range(1, 4):
            arrived(("rq", k), reqs.at[x_at[4 - k]])

    send_requests()
    send_chunk(0)
    send_weights()
    send_chunk(1)
    gram_start()
    transposed(target, tt_own)
    requests_arrived()
    forward_chunk(0)
    send_chunk(2)
    finish_pool(0)
    x_pack(0)
    x_merge(0)
    x_final(0)
    z_start(0)
    gram_second()
    forward_chunk(1)
    send_chunk(3)
    finish_pool(1)
    x_pack(1)
    weights_arrived()
    hess_piece(0, z, start=True)
    x_merge(1)
    z_hop(0, 1)
    x_final(1)
    z_start(1)
    hess_piece(0, z_at[7])
    forward_chunk(2)
    z_hop(0, 2)
    finish_pool(2)
    x_pack(2)
    hess_piece(0, z_at[1])
    x_merge(2)
    gram_third()
    z_hop(0, 3)
    z_hop(1, 1)
    forward_chunk(3)
    x_final(2)
    hess_piece(0, z_at[6])
    finish_pool(3)
    x_pack(3)
    hess_piece(0, z_at[2])
    hess_piece(0, z_at[5])
    x_merge(3)
    z_hop(1, 2)
    z_hop(0, 4)
    hess_piece(0, z_at[3])
    hess_piece(0, z_at[4])
    x_final(3)
    z_hop(1, 3)
    grad_start()
    hess_piece(1, z)
    for k in (7, 1, 6, 2, 5, 3):
        hess_piece(1, z_at[k])
    z_hop(1, 4)
    hess_piece(1, z_at[4])
    send("h", hacc.at[pl.ds((1 - y_hi) * NI, NI)], hin, partner)
    gram_last()
    grad_last()
    arrived("h", hin)
    hess_ref[...] = hacc[pl.ds(y_hi * NI, NI)] + hin[...]
    for copy in sent:
        copy.wait_send()
    assert len(slots) <= NSEM, len(slots)


NSEM = 160


def normal_equations(user_factors, item_factors, tile_user, tile_weight, tile_target):
    vm = pltpu.VMEM
    chunk = (NT, ROWS // 2, KB)
    both = (2,) + chunk
    return pl.pallas_call(
        gather_kernel,
        out_shape=(
            jax.ShapeDtypeStruct((NI, KB, KB), F32),
            jax.ShapeDtypeStruct((NI, KB), F32),
            jax.ShapeDtypeStruct((16, 2, 8, KB), F32),
        ),
        in_specs=[pl.BlockSpec(memory_space=pl.ANY)] * 5,
        out_specs=(pl.BlockSpec(memory_space=pltpu.VMEM),) * 3,
        scratch_shapes=[
            [vm((4, OWN, ROWS, KB), BF16)] * NCH,
            [vm(chunk, BF16)] * NCH,
            [vm(chunk, BF16)] * NCH,
            [vm(both, BF16)] * NCH,
            [vm(both, BF16)] * NCH,
            [vm(chunk, BF16)] * NCH,
            [vm(chunk, BF16)] * NCH,
            [vm(both, BF16)] * NCH,
            [vm(both, BF16)] * NCH,
            [vm((NT, ROWS, KB), BF16)] * NQ,
            [vm((NZ, NT, ROWS, KB), BF16)] * NQ,
            pltpu.SMEM((4, 1, NT), jnp.int32),
            vm((TILE, K), BF16),
            vm((NT, TILE, TILE), BF16),
            vm((NT, TILE, TILE), BF16),
            vm((NZ, 16, NT * TILE), BF16),
            vm((NZ, 16, NT * TILE), BF16),
            vm((NZ, 16, NT * TILE), BF16),
            vm((16, KB, KB), F32),
            vm((NI, KB, KB), F32),
            vm((16, NI, KB), F32),
            vm((16, NI, KB), F32),
            vm((16, 2, 8, KB), F32),
            vm((16, 2, 8, KB), F32),
            vm((2, 8, KB), F32),
            vm((16, 2, 8, KB), F32),
            vm((2, 8, KB), F32),
            vm((16, 2, 8, KB), F32),
            pltpu.SemaphoreType.DMA((NCH + 4,)),
            pltpu.SemaphoreType.DMA((NSEM,)),
            pltpu.SemaphoreType.DMA((NSEM,)),
        ],
        compiler_params=pltpu.CompilerParams(
            collective_id=0, has_side_effects=True, vmem_limit_bytes=48 * 1024 * 1024),
        name="normal_equations",
    )(user_factors, tile_user, item_factors, tile_weight, tile_target)


PANEL = 8
RB = 32


def lane_bcast(v, lane):
    return jnp.broadcast_to(v[:, lane:lane+1], v.shape)

def tree(xs):
    while len(xs) > 1:
        xs = [xs[i] + xs[i+1] if i+1 < len(xs) else xs[i] for i in range(0, len(xs), 2)]
    return xs[0]

def sweep_inverse(d, n):
    g = lambda i, j: d[(i, j) if i <= j else (j, i)]
    for k in range(n):
        inv = 1.0 / g(k, k)
        scaled = {i: g(i, k) * inv for i in range(n) if i != k}
        new = {}
        for i in range(n):
            for j in range(i, n):
                if i == k and j == k:
                    new[(i, j)] = -inv
                elif i == k:
                    new[(i, j)] = scaled[j]
                elif j == k:
                    new[(i, j)] = scaled[i]
                else:
                    new[(i, j)] = d[(i, j)] - scaled[i] * g(j, k)
        d = new
        g = lambda i, j, d=d: d[(i, j) if i <= j else (j, i)]
    return {ij: -v for ij, v in d.items()}

def solve_kernel(hess_ref, grad_ref, gram_ref, item_ref, out_ref, a_ref, dinv_ref):
    lane = lax.broadcasted_iota(jnp.int32, (NI, KB), 1)
    gram_s = gram_ref[:, 0].reshape(KB, KB)
    gram_r = gram_ref[:, 1].reshape(KB, KB)
    item = item_ref[...].astype(F32)
    dims = (((1,), (1,)), ((), ()))
    hi = lax.Precision.HIGHEST
    b = grad_ref[...] + PRIOR * (
        lax.dot_general(item[:, :KB], gram_s, dims, precision=hi, preferred_element_type=F32)
        + lax.dot_general(item[:, KB:], gram_r, dims, precision=hi, preferred_element_type=F32))
    for i in range(NI):
        h = hess_ref[i] + PRIOR * gram_s
        a_ref[pl.ds(i, KB, stride=NI), :] = 0.5 * (h + h.T)
    pairs = [(i, j) for i in range(PANEL) for j in range(i, PANEL)]
    for p in range(KB // PANEL):
        k0 = p * PANEL
        rows = [a_ref[pl.ds((k0 + j) * NI, NI), :] for j in range(PANEL)]
        dinv = sweep_inverse({(i, j): lane_bcast(rows[i], k0 + j) for i, j in pairs}, PANEL)
        for n, ij in enumerate(pairs):
            dinv_ref[p, n] = dinv[ij]
        if p + 1 == KB // PANEL:
            break
        kept = [jnp.where(lane >= k0 + PANEL, r, 0.0) for r in rows]
        ws = [tree([dinv[(min(i, j), max(i, j))] * kept[j] for j in range(PANEL)]) for i in range(PANEL)]
        b = b - tree([lane_bcast(b, k0 + j) * ws[j] for j in range(PANEL)])
        def update(base, count):
            vs = [a_ref[pl.ds(base + q * NI, NI), :] for q in range(count)]
            vs = [v - tree([lane_bcast(v, k0 + j) * ws[j] for j in range(PANEL)]) for v in vs]
            for q in range(count):
                a_ref[pl.ds(base + q * NI, NI), :] = vs[q]
        left = KB - k0 - PANEL
        if left % RB:
            update((k0 + PANEL) * NI, left % RB)
        if left // RB:
            first = (k0 + PANEL + left % RB) // RB
            @pl.loop(first, KB // RB)
            def _(g):
                update(pl.multiple_of(g * (RB * NI), RB * NI), RB)
    x = jnp.zeros((NI, KB), F32)
    for p in range(KB // PANEL - 1, -1, -1):
        k0 = p * PANEL
        bs = [lane_bcast(b, k0 + j) for j in range(PANEL)]
        dinv = {ij: dinv_ref[p, n] for n, ij in enumerate(pairs)}
        xs = [tree([dinv[(min(i, j), max(i, j))] * bs[j] for j in range(PANEL)]) for i in range(PANEL)]
        for j in range(PANEL):
            x = jnp.where(lane == k0 + j, xs[j], x)
        if p:
            b = b - tree([xs[j] * jnp.where(lane < k0, a_ref[pl.ds((k0 + j) * NI, NI), :], 0.0) for j in range(PANEL)])
    out_ref[...] = item[:, :KB] - x

def solve(hess, grad, gram, item):
    return pl.pallas_call(
        solve_kernel,
        out_shape=jax.ShapeDtypeStruct((NI, KB), F32),
        in_specs=[pl.BlockSpec(memory_space=pltpu.VMEM)]*4,
        out_specs=pl.BlockSpec(memory_space=pltpu.VMEM),
        scratch_shapes=[pltpu.VMEM((KB*NI, KB), F32), pltpu.VMEM((KB//PANEL, PANEL*(PANEL+1)//2, NI, KB), F32)],
        name="block_solve",
    )(hess, grad, gram, item)


def local(user_factors, item_factors, tile_user, tile_weight, tile_target):
    hess, grad, gram = normal_equations(
        user_factors.reshape(OWN, TILE, K), item_factors, tile_user[0], tile_weight[0, 0], tile_target[0, 0])
    mine = lax.dynamic_slice_in_dim(item_factors, lax.axis_index("grp") * NI, NI, 0)
    return solve(hess, grad, gram, mine)


def solution(mesh):
    return jax.shard_map(
        local,
        mesh=mesh,
        in_specs=(
            P("grp", "blk", None),
            P("blk", None),
            P("blk", "grp", None),
            P("blk", "grp", None, None, None),
            P("blk", "grp", None, None, None),
        ),
        out_specs=P(("blk", "grp"), None),
        check_vma=False,
    )
```

```python
import functools

import jax
import jax.numpy as jnp
from jax import lax
from jax.experimental import pallas as pl
from jax.experimental.pallas import tpu as pltpu
from jax.sharding import PartitionSpec as P

F32 = jnp.float32
BF16 = jnp.bfloat16
MESH = pl.DeviceIdType.MESH
K = 256
KB = 128
TILE = 128
NT = 8
PRIOR = 0.05
NI = 8
OWN = 16
ROWS = 32
NQ = TILE // ROWS
NCH = 2 * NQ
CU = NT * ROWS
NZ = 8
BOTH_LAST = (((1,), (1,)), ((), ()))
BOTH_FIRST = (((0,), (0,)), ((), ()))


def gather_kernel(
    user_ref, tile_ref, item_ref, weight_ref, target_ref,
    system_ref, rhs_ref, mine_ref,
    pools, far_a, far_b, out_p, out_m, in_a, in_b, in_p, in_m, rights, zbufs,
    reqs, item, itemf, weight, target, wt_own, tt_own, wz, hacc, hsend, hin, hown, gsend, gin,
    gpart, gin1, gone, gin2, gtwo, gall, local_sem, send_sem, recv_sem,
):
    me_b, me_g = lax.axis_index("blk"), lax.axis_index("grp")
    y_lo, x, core = me_b // 8, lax.rem(me_b // 2, 4), lax.rem(me_b, 2)
    z, y_hi = me_g // 2, lax.rem(me_g, 2)
    own = y_lo * 2 + core
    across = (1 - y_lo) * 2 + core
    sibling = (me_b + 1 - 2 * core, me_g)
    y_peer = (lax.rem(me_b + 8, 16), me_g)
    x_at = [lax.rem(x + k, 4) for k in range(4)]
    x_peer = [(y_lo * 8 + x_at[k] * 2 + core, me_g) for k in range(4)]
    z_at = [lax.rem(z + k, NZ) for k in range(NZ)]
    z_peer = [(me_b, z_at[k] * 2 + y_hi) for k in range(NZ)]
    blk_at = [lax.rem(me_b + k, 16) for k in range(16)]
    grp_at = [lax.rem(me_g + k, 16) for k in range(16)]
    blk_peer = [(blk_at[k], me_g) for k in range(16)]
    grp_peer = [(me_b, grp_at[k]) for k in range(16)]
    partner = (me_b, me_g + 1 - 2 * y_hi)

    slots, sent = {}, []

    def slot(name):
        return slots.setdefault(name, len(slots))

    def send(name, src, dst, device):
        k = slot(name)
        copy = pltpu.make_async_remote_copy(
            src_ref=src, dst_ref=dst, send_sem=send_sem.at[k], recv_sem=recv_sem.at[k],
            device_id=device, device_id_type=MESH)
        copy.start()
        sent.append(copy)

    def arrived(name, dst):
        k = slot(name)
        pltpu.make_async_remote_copy(
            src_ref=dst, dst_ref=dst, send_sem=send_sem.at[k], recv_sem=recv_sem.at[k],
            device_id=sibling, device_id_type=MESH).wait_recv()

    locals_ = {}

    def fetch(name, src, dst):
        copy = pltpu.make_async_copy(src, dst, local_sem.at[len(locals_)])
        copy.start()
        locals_[name] = copy

    barrier = pltpu.get_barrier_semaphore()
    for k in range(1, 16):
        pl.semaphore_signal(barrier, inc=1, device_id=blk_peer[k], device_id_type=MESH)
        pl.semaphore_signal(barrier, inc=1, device_id=grp_peer[k], device_id_type=MESH)
    for c in range(NCH):
        rows, cols = (c % NQ) * ROWS, (c // NQ) * KB
        fetch(("pool", c), user_ref.at[:, pl.ds(rows, ROWS), pl.ds(cols, KB)], pools[c].at[own])
    fetch("tile", tile_ref, reqs.at[x])
    fetch("weight", weight_ref, weight)
    fetch("target", target_ref, target)
    fetch("item", item_ref, item)

    for name in [("pool", c) for c in range(NCH)] + ["tile"]:
        locals_[name].wait()
    pl.semaphore_wait(barrier, 30)

    def send_chunk(c):
        send(("y", c), pools[c].at[own], pools[c].at[own], y_peer)
        send(("s", c), pools[c].at[own], pools[c].at[own], sibling)

    def forward_chunk(c):
        arrived(("y", c), pools[c].at[across])
        send(("f", c), pools[c].at[across], pools[c].at[across], sibling)

    def finish_pool(c):
        other = y_lo * 2 + 1 - core
        diagonal = (1 - y_lo) * 2 + 1 - core
        arrived(("s", c), pools[c].at[other])
        arrived(("f", c), pools[c].at[diagonal])

    def wanted(k, j):
        return reqs[x_at[k], 0, j]

    def column(t):
        return jnp.bitwise_and(jnp.right_shift(t, 5), 3)

    def pick(c, t):
        owner = jnp.right_shift(t, 7) * 2 + jnp.bitwise_and(jnp.right_shift(t, 4), 1)
        return pools[c][owner, jnp.bitwise_and(t, 15)]

    half = ROWS // 2

    def x_pack(c):
        for j in range(NT):
            v = pick(c, wanted(2, j))
            far_a[c][j] = v[:half]
            far_b[c][j] = v[half:]
        send(("xa", c), far_a[c], in_a[c], x_peer[1])
        send(("xb", c), far_b[c], in_b[c], x_peer[3])
        for j in range(NT):
            out_p[c][1, j] = pick(c, wanted(1, j))[half:]
            out_m[c][0, j] = pick(c, wanted(3, j))[:half]
        send(("p1", c), out_p[c].at[1], in_m[c].at[1], x_peer[1])
        send(("m0", c), out_m[c].at[0], in_p[c].at[0], x_peer[3])

    def x_merge(c):
        arrived(("xa", c), in_a[c])
        for j in range(NT):
            t = wanted(1, j)
            out_p[c][0, j] = jnp.where(column(t) == x, pick(c, t)[:half], in_a[c][j])
        send(("p0", c), out_p[c].at[0], in_m[c].at[0], x_peer[1])
        arrived(("xb", c), in_b[c])
        for j in range(NT):
            t = wanted(3, j)
            out_m[c][1, j] = jnp.where(column(t) == x, pick(c, t)[half:], in_b[c][j])
        send(("m1", c), out_m[c].at[1], in_p[c].at[1], x_peer[3])

    def x_final(c):
        arrived(("p1", c), in_m[c].at[1])
        arrived(("m0", c), in_p[c].at[0])
        arrived(("p0", c), in_m[c].at[0])
        arrived(("m1", c), in_p[c].at[1])
        for j in range(NT):
            t = wanted(0, j)
            away = jnp.bitwise_and(column(t) - x + 4, 3)
            mine = pick(c, t)
            first = jnp.where(away == 0, mine[:half], jnp.where(away == 1, in_p[c][0, j], in_m[c][0, j]))
            second = jnp.where(away == 0, mine[half:], jnp.where(away == 3, in_m[c][1, j], in_p[c][1, j]))
            if c < NQ:
                zbufs[c][z, j, :half] = first
                zbufs[c][z, j, half:] = second
            else:
                rights[c - NQ][j, :half] = first
                rights[c - NQ][j, half:] = second

    def z_start(q):
        send(("zr", q, 1), zbufs[q].at[z], zbufs[q].at[z], z_peer[1])
        send(("zl", q, 1), zbufs[q].at[z], zbufs[q].at[z], z_peer[7])

    def z_hop(q, h):
        if h < 4:
            from_left, from_right = z_at[NZ - h], z_at[h]
            arrived(("zr", q, h), zbufs[q].at[from_left])
            part = zbufs[q].at[from_left] if h < 3 else zbufs[q].at[from_left, pl.ds(0, NT // 2)]
            send(("zr", q, h + 1), part, part, z_peer[1])
            arrived(("zl", q, h), zbufs[q].at[from_right])
            part = zbufs[q].at[from_right] if h < 3 else zbufs[q].at[from_right, pl.ds(NT // 2, NT // 2)]
            send(("zl", q, h + 1), part, part, z_peer[7])
        else:
            arrived(("zr", q, 4), zbufs[q].at[z_at[4], pl.ds(0, NT // 2)])
            arrived(("zl", q, 4), zbufs[q].at[z_at[4], pl.ds(NT // 2, NT // 2)])

    def transposed(ref, out):
        span = TILE // ROWS
        for q in range(NQ):
            for p in range(NT // span):
                block = ref[p * span:(p + 1) * span, q * ROWS:(q + 1) * ROWS, :].reshape(TILE, TILE)
                out[:, :, pl.ds((q * (NT // span) + p) * TILE, TILE)] = block.T.reshape(NZ, 16, TILE)

    def send_weights():
        locals_["weight"].wait()
        transposed(weight, wt_own)
        for k in range(1, NZ):
            send(("w", k), wt_own.at[z_at[k]], wz.at[z], z_peer[k])
        wz[z] = wt_own[z]

    def weights_arrived():
        for k in range(1, NZ):
            arrived(("w", k), wz.at[z_at[NZ - k]])

    def gram_start():
        left = jnp.zeros((KB, KB), F32)
        right = jnp.zeros((KB, KB), F32)
        for q in range(NQ):
            a = pools[q][own].reshape(OWN * ROWS, KB)
            b = pools[NQ + q][own].reshape(OWN * ROWS, KB)
            left += lax.dot_general(a, a, BOTH_FIRST, preferred_element_type=F32)
            right += lax.dot_general(a, b, BOTH_FIRST, preferred_element_type=F32)
        gpart[:, 0] = left.reshape(16, 8, KB)
        gpart[:, 1] = right.reshape(16, 8, KB)
        for k in range(1, 16):
            send(("g1", k), gpart.at[blk_at[k]], gin1.at[me_b], blk_peer[k])
        gin1[me_b] = gpart[me_b]

    def gram_second():
        for k in range(1, 16):
            arrived(("g1", k), gin1.at[blk_at[16 - k]])
        gone[...] = jnp.sum(gin1[...], axis=0)
        for k in range(1, 16):
            send(("g2", k), gone, gin2.at[me_g], grp_peer[k])
        gin2[me_g] = gone[...]

    def gram_third():
        for k in range(1, 16):
            arrived(("g2", k), gin2.at[grp_at[16 - k]])
        gtwo[...] = jnp.sum(gin2[...], axis=0)
        for k in range(1, 16):
            send(("g3", k), gtwo, gall.at[me_b], blk_peer[k])
        gall[me_b] = gtwo[...]

    def gram_last():
        for k in range(1, 16):
            arrived(("g3", k), gall.at[blk_at[16 - k]])

    GROUP = 4

    def hess_piece(q, sources, start=False, last=False):
        users = [zbufs[q][s].reshape(CU, KB) for s in sources]
        users_t = jnp.concatenate(
            [u[p * KB:(p + 1) * KB].T for u in users for p in range(CU // KB)], axis=1)
        width = CU * len(sources)
        users_t = users_t.reshape(KB // 16, 16, width)
        users = jnp.concatenate(users, axis=0)
        scale = jnp.concatenate([wz[s, :, pl.ds(q * CU, CU)].astype(F32) for s in sources], axis=1)
        theirs = jnp.where(y_hi == 0, scale[8:], scale[:8])
        ours = jnp.where(y_hi == 0, scale[:8], scale[8:])
        scale = jnp.concatenate([theirs, ours], axis=0)
        for i0 in range(0, 16, GROUP):
            lhs = []
            for i in range(i0, i0 + GROUP):
                row = jnp.broadcast_to(scale[i:i + 1], (16, width)).astype(BF16)
                lhs.append((row[None] * users_t).reshape(KB, width))
            part = jnp.dot(jnp.concatenate(lhs, axis=0), users, preferred_element_type=F32)
            part = part.reshape(GROUP, KB, KB)
            if start:
                hacc[i0:i0 + GROUP] = part
            else:
                hacc[i0:i0 + GROUP] += part
            if last and i0 < NI:
                for i in range(i0, i0 + GROUP, 2):
                    fold(i)

    def row_col():
        return (lax.broadcasted_iota(jnp.int32, (KB, KB), 0), lax.broadcasted_iota(jnp.int32, (KB, KB), 1))

    def fold(i):
        row, col = row_col()
        hsend[i // 2, :KB] = jnp.where(row <= col, hacc[i], hacc[i + 1])
        diag = jnp.sum(jnp.where(row == col, hacc[i + 1], 0.0), axis=0, keepdims=True)
        hsend[i // 2, KB:] = jnp.broadcast_to(diag, (8, KB))
        send(("h", i), hsend.at[i // 2], hin.at[i // 2], partner)

    def own_systems():
        prior = PRIOR * gall[:, 0].reshape(KB, KB)
        for i in range(NI):
            h = hacc[NI + i]
            hown[i] = 0.5 * (h + h.T) + prior

    def join_systems():
        row, col = row_col()
        for i in range(0, NI, 2):
            arrived(("h", i), hin.at[i // 2])
            square = hin[i // 2, :KB]
            turned = square.T
            diag = hin[i // 2, KB:KB + 1]
            first = jnp.where(row <= col, square, turned)
            second = jnp.where(row > col, square, jnp.where(row == col, diag, turned))
            system_ref[pl.ds(i, KB, stride=NI), :] = hown[i] + first
            system_ref[pl.ds(i + 1, KB, stride=NI), :] = hown[i + 1] + second

    def grad_start():
        total = jnp.zeros((TILE, KB), F32)
        items = item[...]
        for q in range(NQ):
            left = zbufs[q][z].reshape(CU, KB)
            right = rights[q][...].reshape(CU, KB)
            pred = lax.dot_general(items[:, :KB], left, BOTH_LAST, preferred_element_type=F32)
            pred += lax.dot_general(items[:, KB:], right, BOTH_LAST, preferred_element_type=F32)
            w = wt_own[:, :, pl.ds(q * CU, CU)].reshape(TILE, CU).astype(F32)
            t = tt_own[:, :, pl.ds(q * CU, CU)].reshape(TILE, CU).astype(F32)
            resid = (w * (pred - t)).astype(BF16)
            total += jnp.dot(resid, left, preferred_element_type=F32)
        gsend[...] = total.reshape(16, NI, KB)
        for k in range(1, 16):
            send(("gr", k), gsend.at[grp_at[k]], gin.at[me_g], grp_peer[k])
        gin[me_g] = gsend[me_g]

    def rhs_start():
        itemf[...] = item[...].astype(F32)
        mine = itemf[pl.ds(me_g * NI, NI), :]
        mine_ref[...] = mine[:, :KB]
        exact = lax.Precision.HIGHEST
        rhs_ref[...] = PRIOR * (
            lax.dot_general(mine[:, :KB], gall[:, 0].reshape(KB, KB), BOTH_LAST,
                            precision=exact, preferred_element_type=F32)
            + lax.dot_general(mine[:, KB:], gall[:, 1].reshape(KB, KB), BOTH_LAST,
                              precision=exact, preferred_element_type=F32))

    def grad_last():
        for k in range(1, 16):
            arrived(("gr", k), gin.at[grp_at[16 - k]])
        rhs_ref[...] += jnp.sum(gin[...], axis=0)

    def target_ready():
        locals_["target"].wait()
        transposed(target, tt_own)
        locals_["item"].wait()

    def send_requests():
        for k in range(1, 4):
            send(("rq", k), reqs.at[x], reqs.at[x], x_peer[k])

    def requests_arrived():
        for k in range(1, 4):
            arrived(("rq", k), reqs.at[x_at[4 - k]])

    send_requests()
    send_chunk(0)
    send_chunk(1)
    send_chunk(2)
    send_weights()
    gram_start()
    target_ready()
    requests_arrived()
    forward_chunk(0)
    send_chunk(3)
    finish_pool(0)
    x_pack(0)
    gram_second()
    forward_chunk(1)
    send_chunk(4)
    x_merge(0)
    finish_pool(1)
    x_pack(1)
    forward_chunk(2)
    send_chunk(5)
    x_final(0)
    z_start(0)
    weights_arrived()
    x_merge(1)
    finish_pool(2)
    x_pack(2)
    gram_third()
    forward_chunk(3)
    send_chunk(6)
    z_hop(0, 1)
    x_final(1)
    z_start(1)
    x_merge(2)
    hess_piece(0, (z_at[7], z_at[1]), start=True)
    finish_pool(3)
    x_pack(3)
    forward_chunk(4)
    send_chunk(7)
    z_hop(0, 2)
    z_hop(1, 1)
    x_final(2)
    z_start(2)
    hess_piece(0, (z_at[6], z_at[2]))
    x_merge(3)
    hess_piece(1, (z_at[7], z_at[1]))
    finish_pool(4)
    x_pack(4)
    forward_chunk(5)
    z_hop(0, 3)
    z_hop(1, 2)
    z_hop(2, 1)
    hess_piece(0, (z_at[5], z_at[3]))
    x_final(3)
    z_start(3)
    hess_piece(1, (z_at[6], z_at[2]))
    x_merge(4)
    hess_piece(2, (z_at[7], z_at[1]))
    finish_pool(5)
    x_pack(5)
    gram_last()
    rhs_start()
    forward_chunk(6)
    z_hop(0, 4)
    z_hop(1, 3)
    z_hop(2, 2)
    hess_piece(0, (z, z_at[4]))
    z_hop(3, 1)
    hess_piece(1, (z_at[5], z_at[3]))
    x_final(4)
    hess_piece(2, (z_at[6], z_at[2]))
    x_merge(5)
    hess_piece(3, (z_at[7], z_at[1]))
    finish_pool(6)
    x_pack(6)
    forward_chunk(7)
    z_hop(1, 4)
    z_hop(2, 3)
    z_hop(3, 2)
    hess_piece(1, (z, z_at[4]))
    hess_piece(2, (z_at[5], z_at[3]))
    x_final(5)
    hess_piece(3, (z_at[6], z_at[2]))
    x_merge(6)
    finish_pool(7)
    x_pack(7)
    z_hop(2, 4)
    z_hop(3, 3)
    hess_piece(2, (z, z_at[4]))
    hess_piece(3, (z_at[5], z_at[3]))
    x_final(6)
    x_merge(7)
    z_hop(3, 4)
    hess_piece(3, (z, z_at[4]), last=True)
    x_final(7)
    grad_start()
    own_systems()
    grad_last()
    join_systems()
    for copy in sent:
        copy.wait_send()
    assert len(slots) <= NSEM, len(slots)


NSEM = 260


def normal_equations(user_factors, item_factors, tile_user, tile_weight, tile_target):
    vm = pltpu.VMEM
    chunk = (NT, ROWS // 2, KB)
    both = (2,) + chunk
    return pl.pallas_call(
        gather_kernel,
        out_shape=(
            jax.ShapeDtypeStruct((KB * NI, KB), F32),
            jax.ShapeDtypeStruct((NI, KB), F32),
            jax.ShapeDtypeStruct((NI, KB), F32),
        ),
        in_specs=[pl.BlockSpec(memory_space=pl.ANY)] * 5,
        out_specs=(pl.BlockSpec(memory_space=pltpu.VMEM),) * 3,
        scratch_shapes=[
            [vm((4, OWN, ROWS, KB), BF16)] * NCH,
            [vm(chunk, BF16)] * NCH,
            [vm(chunk, BF16)] * NCH,
            [vm(both, BF16)] * NCH,
            [vm(both, BF16)] * NCH,
            [vm(chunk, BF16)] * NCH,
            [vm(chunk, BF16)] * NCH,
            [vm(both, BF16)] * NCH,
            [vm(both, BF16)] * NCH,
            [vm((NT, ROWS, KB), BF16)] * NQ,
            [vm((NZ, NT, ROWS, KB), BF16)] * NQ,
            pltpu.SMEM((4, 1, NT), jnp.int32),
            vm((TILE, K), BF16),
            vm((TILE, K), F32),
            vm((NT, TILE, TILE), BF16),
            vm((NT, TILE, TILE), BF16),
            vm((NZ, 16, NT * TILE), BF16),
            vm((NZ, 16, NT * TILE), BF16),
            vm((NZ, 16, NT * TILE), BF16),
            vm((16, KB, KB), F32),
            vm((NI // 2, KB + 8, KB), F32),
            vm((NI // 2, KB + 8, KB), F32),
            vm((NI, KB, KB), F32),
            vm((16, NI, KB), F32),
            vm((16, NI, KB), F32),
            vm((16, 2, 8, KB), F32),
            vm((16, 2, 8, KB), F32),
            vm((2, 8, KB), F32),
            vm((16, 2, 8, KB), F32),
            vm((2, 8, KB), F32),
            vm((16, 2, 8, KB), F32),
            pltpu.SemaphoreType.DMA((NCH + 4,)),
            pltpu.SemaphoreType.DMA((NSEM,)),
            pltpu.SemaphoreType.DMA((NSEM,)),
        ],
        compiler_params=pltpu.CompilerParams(
            collective_id=0, has_side_effects=True, vmem_limit_bytes=60 * 1024 * 1024),
        name="normal_equations",
    )(user_factors, tile_user, item_factors, tile_weight, tile_target)


PANEL = 8
RB = 32


def lane_bcast(v, lane):
    return jnp.broadcast_to(v[:, lane:lane+1], v.shape)

def tree(xs):
    while len(xs) > 1:
        xs = [xs[i] + xs[i+1] if i+1 < len(xs) else xs[i] for i in range(0, len(xs), 2)]
    return xs[0]

def sweep_inverse(d, n):
    g = lambda i, j: d[(i, j) if i <= j else (j, i)]
    for k in range(n):
        inv = 1.0 / g(k, k)
        scaled = {i: g(i, k) * inv for i in range(n) if i != k}
        new = {}
        for i in range(n):
            for j in range(i, n):
                if i == k and j == k:
                    new[(i, j)] = -inv
                elif i == k:
                    new[(i, j)] = scaled[j]
                elif j == k:
                    new[(i, j)] = scaled[i]
                else:
                    new[(i, j)] = d[(i, j)] - scaled[i] * g(j, k)
        d = new
        g = lambda i, j, d=d: d[(i, j) if i <= j else (j, i)]
    return {ij: -v for ij, v in d.items()}

def solve_kernel(system_ref, rhs_ref, mine_ref, out_ref, a_ref, dinv_ref, sem):
    load = pltpu.make_async_copy(system_ref, a_ref, sem)
    load.start()
    lane = lax.broadcasted_iota(jnp.int32, (NI, KB), 1)
    b = rhs_ref[...]
    load.wait()
    pairs = [(i, j) for i in range(PANEL) for j in range(i, PANEL)]
    for p in range(KB // PANEL):
        k0 = p * PANEL
        rows = [a_ref[pl.ds((k0 + j) * NI, NI), :] for j in range(PANEL)]
        dinv = sweep_inverse({(i, j): lane_bcast(rows[i], k0 + j) for i, j in pairs}, PANEL)
        for n, ij in enumerate(pairs):
            dinv_ref[p, n] = dinv[ij]
        if p + 1 == KB // PANEL:
            break
        kept = [jnp.where(lane >= k0 + PANEL, r, 0.0) for r in rows]
        ws = [tree([dinv[(min(i, j), max(i, j))] * kept[j] for j in range(PANEL)]) for i in range(PANEL)]
        b = b - tree([lane_bcast(b, k0 + j) * ws[j] for j in range(PANEL)])
        def update(base, count):
            vs = [a_ref[pl.ds(base + q * NI, NI), :] for q in range(count)]
            vs = [v - tree([lane_bcast(v, k0 + j) * ws[j] for j in range(PANEL)]) for v in vs]
            for q in range(count):
                a_ref[pl.ds(base + q * NI, NI), :] = vs[q]
        left = KB - k0 - PANEL
        if left % RB:
            update((k0 + PANEL) * NI, left % RB)
        if left // RB:
            first = (k0 + PANEL + left % RB) // RB
            @pl.loop(first, KB // RB)
            def _(g):
                update(pl.multiple_of(g * (RB * NI), RB * NI), RB)
    x = jnp.zeros((NI, KB), F32)
    for p in range(KB // PANEL - 1, -1, -1):
        k0 = p * PANEL
        bs = [lane_bcast(b, k0 + j) for j in range(PANEL)]
        dinv = {ij: dinv_ref[p, n] for n, ij in enumerate(pairs)}
        xs = [tree([dinv[(min(i, j), max(i, j))] * bs[j] for j in range(PANEL)]) for i in range(PANEL)]
        for j in range(PANEL):
            x = jnp.where(lane == k0 + j, xs[j], x)
        if p:
            b = b - tree([xs[j] * jnp.where(lane < k0, a_ref[pl.ds((k0 + j) * NI, NI), :], 0.0) for j in range(PANEL)])
    out_ref[...] = mine_ref[...] - x

def solve(system, rhs, mine):
    vmem = pl.BlockSpec(memory_space=pltpu.VMEM)
    return pl.pallas_call(
        solve_kernel,
        out_shape=jax.ShapeDtypeStruct((NI, KB), F32),
        in_specs=[pl.BlockSpec(memory_space=pl.ANY), vmem, vmem],
        out_specs=vmem,
        scratch_shapes=[
            pltpu.VMEM((KB * NI, KB), F32),
            pltpu.VMEM((KB // PANEL, PANEL * (PANEL + 1) // 2, NI, KB), F32),
            pltpu.SemaphoreType.DMA,
        ],
        compiler_params=pltpu.CompilerParams(vmem_limit_bytes=60 * 1024 * 1024),
        name="block_solve",
    )(system, rhs, mine)


def local(user_factors, item_factors, tile_user, tile_weight, tile_target):
    return solve(*normal_equations(
        user_factors.reshape(OWN, TILE, K), item_factors, tile_user[0], tile_weight[0, 0], tile_target[0, 0]))


def solution(mesh):
    return jax.shard_map(
        local,
        mesh=mesh,
        in_specs=(
            P("grp", "blk", None),
            P("blk", None),
            P("blk", "grp", None),
            P("blk", "grp", None, None, None),
            P("blk", "grp", None, None, None),
        ),
        out_specs=P(("blk", "grp"), None),
        check_vma=False,
    )
```

```python
import functools

import jax
import jax.numpy as jnp
from jax import lax
from jax.experimental import pallas as pl
from jax.experimental.pallas import tpu as pltpu
from jax.sharding import PartitionSpec as P

F32 = jnp.float32
BF16 = jnp.bfloat16
MESH = pl.DeviceIdType.MESH
K = 256
KB = 128
TILE = 128
NT = 8
PRIOR = 0.05
NI = 8
OWN = 16
ROWS = 32
NQ = TILE // ROWS
NCH = 2 * NQ
CU = NT * ROWS
NZ = 8
BOTH_LAST = (((1,), (1,)), ((), ()))
BOTH_FIRST = (((0,), (0,)), ((), ()))


def gather_kernel(
    user_ref, tile_ref, item_ref, weight_ref, target_ref,
    system_ref, rhs_ref, mine_ref,
    pools, far_a, far_b, out_p, out_m, in_a, in_b, in_p, in_m, rights, zbufs,
    reqs, item, itemf, weight, target, wt_own, tt_own, wz, hacc, hsend, hin, hown, gsend, gin,
    gpart, gin1, gone, gin2, gtwo, gall, local_sem, send_sem, recv_sem,
):
    me_b, me_g = lax.axis_index("blk"), lax.axis_index("grp")
    y_lo, x, core = me_b // 8, lax.rem(me_b // 2, 4), lax.rem(me_b, 2)
    z, y_hi = me_g // 2, lax.rem(me_g, 2)
    own = y_lo * 2 + core
    across = (1 - y_lo) * 2 + core
    sibling = (me_b + 1 - 2 * core, me_g)
    y_peer = (lax.rem(me_b + 8, 16), me_g)
    x_at = [lax.rem(x + k, 4) for k in range(4)]
    x_peer = [(y_lo * 8 + x_at[k] * 2 + core, me_g) for k in range(4)]
    z_at = [lax.rem(z + k, NZ) for k in range(NZ)]
    z_peer = [(me_b, z_at[k] * 2 + y_hi) for k in range(NZ)]
    blk_at = [lax.rem(me_b + k, 16) for k in range(16)]
    grp_at = [lax.rem(me_g + k, 16) for k in range(16)]
    blk_peer = [(blk_at[k], me_g) for k in range(16)]
    grp_peer = [(me_b, grp_at[k]) for k in range(16)]
    partner = (me_b, me_g + 1 - 2 * y_hi)

    slots, sent = {}, []

    def slot(name):
        return slots.setdefault(name, len(slots))

    def send(name, src, dst, device):
        k = slot(name)
        copy = pltpu.make_async_remote_copy(
            src_ref=src, dst_ref=dst, send_sem=send_sem.at[k], recv_sem=recv_sem.at[k],
            device_id=device, device_id_type=MESH)
        copy.start()
        sent.append(copy)

    def arrived(name, dst):
        k = slot(name)
        pltpu.make_async_remote_copy(
            src_ref=dst, dst_ref=dst, send_sem=send_sem.at[k], recv_sem=recv_sem.at[k],
            device_id=sibling, device_id_type=MESH).wait_recv()

    locals_ = {}

    def fetch(name, src, dst):
        copy = pltpu.make_async_copy(src, dst, local_sem.at[len(locals_)])
        copy.start()
        locals_[name] = copy

    barrier = pltpu.get_barrier_semaphore()
    for k in range(1, 16):
        pl.semaphore_signal(barrier, inc=1, device_id=blk_peer[k], device_id_type=MESH)
        pl.semaphore_signal(barrier, inc=1, device_id=grp_peer[k], device_id_type=MESH)
    for c in range(NCH):
        rows, cols = (c % NQ) * ROWS, (c // NQ) * KB
        fetch(("pool", c), user_ref.at[:, pl.ds(rows, ROWS), pl.ds(cols, KB)], pools[c].at[own])
    fetch("tile", tile_ref, reqs.at[x])
    fetch("weight", weight_ref, weight)
    fetch("target", target_ref, target)
    fetch("item", item_ref, item)

    for name in [("pool", c) for c in range(NCH)] + ["tile"]:
        locals_[name].wait()
    pl.semaphore_wait(barrier, 30)

    def send_chunk(c):
        send(("y", c), pools[c].at[own], pools[c].at[own], y_peer)
        send(("s", c), pools[c].at[own], pools[c].at[own], sibling)

    def forward_chunk(c):
        arrived(("y", c), pools[c].at[across])
        send(("f", c), pools[c].at[across], pools[c].at[across], sibling)

    def finish_pool(c):
        other = y_lo * 2 + 1 - core
        diagonal = (1 - y_lo) * 2 + 1 - core
        arrived(("s", c), pools[c].at[other])
        arrived(("f", c), pools[c].at[diagonal])

    def wanted(k, j):
        return reqs[x_at[k], 0, j]

    def column(t):
        return jnp.bitwise_and(jnp.right_shift(t, 5), 3)

    def pick(c, t):
        owner = jnp.right_shift(t, 7) * 2 + jnp.bitwise_and(jnp.right_shift(t, 4), 1)
        return pools[c][owner, jnp.bitwise_and(t, 15)]

    half = ROWS // 2

    def x_pack(c):
        for j in range(NT):
            v = pick(c, wanted(2, j))
            far_a[c][j] = v[:half]
            far_b[c][j] = v[half:]
        send(("xa", c), far_a[c], in_a[c], x_peer[1])
        send(("xb", c), far_b[c], in_b[c], x_peer[3])
        for j in range(NT):
            out_p[c][1, j] = pick(c, wanted(1, j))[half:]
            out_m[c][0, j] = pick(c, wanted(3, j))[:half]
        send(("p1", c), out_p[c].at[1], in_m[c].at[1], x_peer[1])
        send(("m0", c), out_m[c].at[0], in_p[c].at[0], x_peer[3])

    def x_merge(c):
        arrived(("xa", c), in_a[c])
        for j in range(NT):
            t = wanted(1, j)
            out_p[c][0, j] = jnp.where(column(t) == x, pick(c, t)[:half], in_a[c][j])
        send(("p0", c), out_p[c].at[0], in_m[c].at[0], x_peer[1])
        arrived(("xb", c), in_b[c])
        for j in range(NT):
            t = wanted(3, j)
            out_m[c][1, j] = jnp.where(column(t) == x, pick(c, t)[half:], in_b[c][j])
        send(("m1", c), out_m[c].at[1], in_p[c].at[1], x_peer[3])

    def x_final(c):
        arrived(("p1", c), in_m[c].at[1])
        arrived(("m0", c), in_p[c].at[0])
        arrived(("p0", c), in_m[c].at[0])
        arrived(("m1", c), in_p[c].at[1])
        for j in range(NT):
            t = wanted(0, j)
            away = jnp.bitwise_and(column(t) - x + 4, 3)
            mine = pick(c, t)
            first = jnp.where(away == 0, mine[:half], jnp.where(away == 1, in_p[c][0, j], in_m[c][0, j]))
            second = jnp.where(away == 0, mine[half:], jnp.where(away == 3, in_m[c][1, j], in_p[c][1, j]))
            put(c, j, first, second)

    def x_pack_direct(c):
        for j in range(NT):
            v = pick(c, wanted(2, j))
            far_a[c][j] = v[:half]
            far_b[c][j] = v[half:]
        send(("xa", c), far_a[c], in_a[c], x_peer[2])
        send(("xb", c), far_b[c], in_b[c], x_peer[2])
        for j in range(NT):
            v = pick(c, wanted(1, j))
            out_p[c][0, j] = v[:half]
            out_p[c][1, j] = v[half:]
            v = pick(c, wanted(3, j))
            out_m[c][0, j] = v[:half]
            out_m[c][1, j] = v[half:]
        send(("p0", c), out_p[c], in_m[c], x_peer[1])
        send(("m0", c), out_m[c], in_p[c], x_peer[3])

    def x_final_direct(c):
        arrived(("p0", c), in_m[c])
        arrived(("m0", c), in_p[c])
        arrived(("xa", c), in_a[c])
        arrived(("xb", c), in_b[c])
        for j in range(NT):
            t = wanted(0, j)
            away = jnp.bitwise_and(column(t) - x + 4, 3)
            mine = pick(c, t)
            parts = []
            for p, far in ((0, in_a[c][j]), (1, in_b[c][j])):
                near = jnp.where(away == 1, in_p[c][p, j], in_m[c][p, j])
                parts.append(jnp.where(away == 0, mine[p * half:(p + 1) * half], jnp.where(away == 2, far, near)))
            put(c, j, *parts)

    def put(c, j, first, second):
        if c < NQ:
            zbufs[c][z, j, :half] = first
            zbufs[c][z, j, half:] = second
        else:
            rights[c - NQ][j, :half] = first
            rights[c - NQ][j, half:] = second

    def z_start(q):
        send(("zr", q, 1), zbufs[q].at[z], zbufs[q].at[z], z_peer[1])
        send(("zl", q, 1), zbufs[q].at[z], zbufs[q].at[z], z_peer[7])

    def z_hop(q, h):
        if h < 4:
            from_left, from_right = z_at[NZ - h], z_at[h]
            arrived(("zr", q, h), zbufs[q].at[from_left])
            part = zbufs[q].at[from_left] if h < 3 else zbufs[q].at[from_left, pl.ds(0, NT // 2)]
            send(("zr", q, h + 1), part, part, z_peer[1])
            arrived(("zl", q, h), zbufs[q].at[from_right])
            part = zbufs[q].at[from_right] if h < 3 else zbufs[q].at[from_right, pl.ds(NT // 2, NT // 2)]
            send(("zl", q, h + 1), part, part, z_peer[7])
        else:
            arrived(("zr", q, 4), zbufs[q].at[z_at[4], pl.ds(0, NT // 2)])
            arrived(("zl", q, 4), zbufs[q].at[z_at[4], pl.ds(NT // 2, NT // 2)])

    def transposed(ref, out):
        span = TILE // ROWS
        for q in range(NQ):
            for p in range(NT // span):
                block = ref[p * span:(p + 1) * span, q * ROWS:(q + 1) * ROWS, :].reshape(TILE, TILE)
                out[:, :, pl.ds((q * (NT // span) + p) * TILE, TILE)] = block.T.reshape(NZ, 16, TILE)

    def send_weights():
        locals_["weight"].wait()
        transposed(weight, wt_own)
        for k in range(1, NZ):
            send(("w", k), wt_own.at[z_at[k]], wz.at[z], z_peer[k])
        wz[z] = wt_own[z]

    def weights_arrived():
        for k in range(1, NZ):
            arrived(("w", k), wz.at[z_at[NZ - k]])

    def gram_start():
        left = jnp.zeros((KB, KB), F32)
        right = jnp.zeros((KB, KB), F32)
        for q in range(NQ):
            a = pools[q][own].reshape(OWN * ROWS, KB)
            b = pools[NQ + q][own].reshape(OWN * ROWS, KB)
            left += lax.dot_general(a, a, BOTH_FIRST, preferred_element_type=F32)
            right += lax.dot_general(a, b, BOTH_FIRST, preferred_element_type=F32)
        gpart[:, 0] = left.reshape(16, 8, KB)
        gpart[:, 1] = right.reshape(16, 8, KB)
        for k in range(1, 16):
            send(("g1", k), gpart.at[blk_at[k]], gin1.at[me_b], blk_peer[k])
        gin1[me_b] = gpart[me_b]

    def gram_second():
        for k in range(1, 16):
            arrived(("g1", k), gin1.at[blk_at[16 - k]])
        gone[...] = jnp.sum(gin1[...], axis=0)
        for k in range(1, 16):
            send(("g2", k), gone, gin2.at[me_g], grp_peer[k])
        gin2[me_g] = gone[...]

    def gram_third():
        for k in range(1, 16):
            arrived(("g2", k), gin2.at[grp_at[16 - k]])
        gtwo[...] = jnp.sum(gin2[...], axis=0)
        for k in range(1, 16):
            send(("g3", k), gtwo, gall.at[me_b], blk_peer[k])
        gall[me_b] = gtwo[...]

    def gram_last():
        for k in range(1, 16):
            arrived(("g3", k), gall.at[blk_at[16 - k]])

    GROUP = 4

    def hess_piece(q, sources, start=False, last=False):
        users = [zbufs[q][s].reshape(CU, KB) for s in sources]
        users_t = jnp.concatenate(
            [u[p * KB:(p + 1) * KB].T for u in users for p in range(CU // KB)], axis=1)
        width = CU * len(sources)
        users_t = users_t.reshape(KB // 16, 16, width)
        users = jnp.concatenate(users, axis=0)
        scale = jnp.concatenate([wz[s, :, pl.ds(q * CU, CU)].astype(F32) for s in sources], axis=1)
        theirs = jnp.where(y_hi == 0, scale[8:], scale[:8])
        ours = jnp.where(y_hi == 0, scale[:8], scale[8:])
        scale = jnp.concatenate([theirs, ours], axis=0)
        for i0 in range(0, 16, GROUP):
            lhs = []
            for i in range(i0, i0 + GROUP):
                row = jnp.broadcast_to(scale[i:i + 1], (16, width)).astype(BF16)
                lhs.append((row[None] * users_t).reshape(KB, width))
            part = jnp.dot(jnp.concatenate(lhs, axis=0), users, preferred_element_type=F32)
            part = part.reshape(GROUP, KB, KB)
            if start:
                hacc[i0:i0 + GROUP] = part
            else:
                hacc[i0:i0 + GROUP] += part
            if last and i0 < NI:
                for i in range(i0, i0 + GROUP, 2):
                    fold(i)

    def row_col():
        return (lax.broadcasted_iota(jnp.int32, (KB, KB), 0), lax.broadcasted_iota(jnp.int32, (KB, KB), 1))

    def fold(i):
        row, col = row_col()
        hsend[i // 2, :KB] = jnp.where(row <= col, hacc[i], hacc[i + 1])
        diag = jnp.sum(jnp.where(row == col, hacc[i + 1], 0.0), axis=0, keepdims=True)
        hsend[i // 2, KB:] = jnp.broadcast_to(diag, (8, KB))
        send(("h", i), hsend.at[i // 2], hin.at[i // 2], partner)

    def own_systems():
        prior = PRIOR * gall[:, 0].reshape(KB, KB)
        for i in range(NI):
            h = hacc[NI + i]
            hown[i] = 0.5 * (h + h.T) + prior

    def join_systems():
        row, col = row_col()
        for i in range(0, NI, 2):
            arrived(("h", i), hin.at[i // 2])
            square = hin[i // 2, :KB]
            turned = square.T
            diag = hin[i // 2, KB:KB + 1]
            first = jnp.where(row <= col, square, turned)
            second = jnp.where(row > col, square, jnp.where(row == col, diag, turned))
            system_ref[pl.ds(i, KB, stride=NI), :] = hown[i] + first
            system_ref[pl.ds(i + 1, KB, stride=NI), :] = hown[i + 1] + second

    def grad_start():
        total = jnp.zeros((TILE, KB), F32)
        items = item[...]
        for q in range(NQ):
            left = zbufs[q][z].reshape(CU, KB)
            right = rights[q][...].reshape(CU, KB)
            pred = lax.dot_general(items[:, :KB], left, BOTH_LAST, preferred_element_type=F32)
            pred += lax.dot_general(items[:, KB:], right, BOTH_LAST, preferred_element_type=F32)
            w = wt_own[:, :, pl.ds(q * CU, CU)].reshape(TILE, CU).astype(F32)
            t = tt_own[:, :, pl.ds(q * CU, CU)].reshape(TILE, CU).astype(F32)
            resid = (w * (pred - t)).astype(BF16)
            total += jnp.dot(resid, left, preferred_element_type=F32)
        gsend[...] = total.reshape(16, NI, KB)
        for k in range(1, 16):
            send(("gr", k), gsend.at[grp_at[k]], gin.at[me_g], grp_peer[k])
        gin[me_g] = gsend[me_g]

    def rhs_start():
        itemf[...] = item[...].astype(F32)
        mine = itemf[pl.ds(me_g * NI, NI), :]
        mine_ref[...] = mine[:, :KB]
        exact = lax.Precision.HIGHEST
        rhs_ref[...] = PRIOR * (
            lax.dot_general(mine[:, :KB], gall[:, 0].reshape(KB, KB), BOTH_LAST,
                            precision=exact, preferred_element_type=F32)
            + lax.dot_general(mine[:, KB:], gall[:, 1].reshape(KB, KB), BOTH_LAST,
                              precision=exact, preferred_element_type=F32))

    def grad_last():
        for k in range(1, 16):
            arrived(("gr", k), gin.at[grp_at[16 - k]])
        rhs_ref[...] += jnp.sum(gin[...], axis=0)

    def target_ready():
        locals_["target"].wait()
        transposed(target, tt_own)
        locals_["item"].wait()

    def send_requests():
        for k in range(1, 4):
            send(("rq", k), reqs.at[x], reqs.at[x], x_peer[k])

    def requests_arrived():
        for k in range(1, 4):
            arrived(("rq", k), reqs.at[x_at[4 - k]])

    send_requests()
    send_chunk(0)
    send_chunk(1)
    send_chunk(2)
    send_weights()
    gram_start()
    target_ready()
    forward_chunk(0)
    send_chunk(3)
    requests_arrived()
    finish_pool(0)
    x_pack_direct(0)
    forward_chunk(1)
    send_chunk(4)
    weights_arrived()
    finish_pool(1)
    x_pack_direct(1)
    forward_chunk(2)
    send_chunk(5)
    gram_second()
    finish_pool(2)
    x_pack_direct(2)
    x_final_direct(0)
    z_start(0)
    forward_chunk(3)
    send_chunk(6)
    finish_pool(3)
    x_pack_direct(3)
    x_final_direct(1)
    z_start(1)
    forward_chunk(4)
    send_chunk(7)
    z_hop(0, 1)
    hess_piece(0, (z_at[7], z_at[1]), start=True)
    finish_pool(4)
    x_pack(4)
    x_final_direct(2)
    z_start(2)
    forward_chunk(5)
    z_hop(1, 1)
    hess_piece(1, (z_at[7], z_at[1]))
    gram_third()
    z_hop(0, 2)
    hess_piece(0, (z_at[6], z_at[2]))
    finish_pool(5)
    x_pack(5)
    forward_chunk(6)
    x_merge(4)
    x_final_direct(3)
    z_start(3)
    z_hop(2, 1)
    hess_piece(2, (z_at[7], z_at[1]))
    z_hop(1, 2)
    hess_piece(1, (z_at[6], z_at[2]))
    finish_pool(6)
    x_pack(6)
    forward_chunk(7)
    x_merge(5)
    z_hop(0, 3)
    hess_piece(0, (z_at[5], z_at[3]))
    x_final(4)
    z_hop(3, 1)
    hess_piece(3, (z_at[7], z_at[1]))
    finish_pool(7)
    x_pack(7)
    x_merge(6)
    z_hop(2, 2)
    hess_piece(2, (z_at[6], z_at[2]))
    x_final(5)
    gram_last()
    rhs_start()
    z_hop(1, 3)
    hess_piece(1, (z_at[5], z_at[3]))
    x_merge(7)
    z_hop(0, 4)
    hess_piece(0, (z, z_at[4]))
    z_hop(3, 2)
    hess_piece(3, (z_at[6], z_at[2]))
    x_final(6)
    z_hop(2, 3)
    hess_piece(2, (z_at[5], z_at[3]))
    x_final(7)
    z_hop(1, 4)
    grad_start()
    z_hop(3, 3)
    hess_piece(1, (z, z_at[4]))
    z_hop(2, 4)
    hess_piece(3, (z_at[5], z_at[3]))
    hess_piece(2, (z, z_at[4]))
    z_hop(3, 4)
    hess_piece(3, (z, z_at[4]), last=True)
    own_systems()
    grad_last()
    join_systems()
    for copy in sent:
        copy.wait_send()
    assert len(slots) <= NSEM, len(slots)


NSEM = 260


def normal_equations(user_factors, item_factors, tile_user, tile_weight, tile_target):
    vm = pltpu.VMEM
    chunk = (NT, ROWS // 2, KB)
    both = (2,) + chunk
    return pl.pallas_call(
        gather_kernel,
        out_shape=(
            jax.ShapeDtypeStruct((KB * NI, KB), F32),
            jax.ShapeDtypeStruct((NI, KB), F32),
            jax.ShapeDtypeStruct((NI, KB), F32),
        ),
        in_specs=[pl.BlockSpec(memory_space=pl.ANY)] * 5,
        out_specs=(pl.BlockSpec(memory_space=pltpu.VMEM),) * 3,
        scratch_shapes=[
            [vm((4, OWN, ROWS, KB), BF16)] * NCH,
            [vm(chunk, BF16)] * NCH,
            [vm(chunk, BF16)] * NCH,
            [vm(both, BF16)] * NCH,
            [vm(both, BF16)] * NCH,
            [vm(chunk, BF16)] * NCH,
            [vm(chunk, BF16)] * NCH,
            [vm(both, BF16)] * NCH,
            [vm(both, BF16)] * NCH,
            [vm((NT, ROWS, KB), BF16)] * NQ,
            [vm((NZ, NT, ROWS, KB), BF16)] * NQ,
            pltpu.SMEM((4, 1, NT), jnp.int32),
            vm((TILE, K), BF16),
            vm((TILE, K), F32),
            vm((NT, TILE, TILE), BF16),
            vm((NT, TILE, TILE), BF16),
            vm((NZ, 16, NT * TILE), BF16),
            vm((NZ, 16, NT * TILE), BF16),
            vm((NZ, 16, NT * TILE), BF16),
            vm((16, KB, KB), F32),
            vm((NI // 2, KB + 8, KB), F32),
            vm((NI // 2, KB + 8, KB), F32),
            vm((NI, KB, KB), F32),
            vm((16, NI, KB), F32),
            vm((16, NI, KB), F32),
            vm((16, 2, 8, KB), F32),
            vm((16, 2, 8, KB), F32),
            vm((2, 8, KB), F32),
            vm((16, 2, 8, KB), F32),
            vm((2, 8, KB), F32),
            vm((16, 2, 8, KB), F32),
            pltpu.SemaphoreType.DMA((NCH + 4,)),
            pltpu.SemaphoreType.DMA((NSEM,)),
            pltpu.SemaphoreType.DMA((NSEM,)),
        ],
        compiler_params=pltpu.CompilerParams(
            collective_id=0, has_side_effects=True, vmem_limit_bytes=60 * 1024 * 1024),
        name="normal_equations",
    )(user_factors, tile_user, item_factors, tile_weight, tile_target)


PANEL = 8


def lane_bcast(v, lane):
    return jnp.broadcast_to(v[:, lane:lane+1], v.shape)

def tree(xs):
    while len(xs) > 1:
        xs = [xs[i] + xs[i+1] if i+1 < len(xs) else xs[i] for i in range(0, len(xs), 2)]
    return xs[0]

def split(v):
    h = v.astype(BF16)
    rest = v - h.astype(F32)
    m = rest.astype(BF16)
    return h, m, (rest - m.astype(F32)).astype(BF16)


def sweep_inverse(d, n):
    g = lambda i, j: d[(i, j) if i <= j else (j, i)]
    for k in range(n):
        inv = 1.0 / g(k, k)
        scaled = {i: g(i, k) * inv for i in range(n) if i != k}
        new = {}
        for i in range(n):
            for j in range(i, n):
                if i == k and j == k:
                    new[(i, j)] = -inv
                elif i == k:
                    new[(i, j)] = scaled[j]
                elif j == k:
                    new[(i, j)] = scaled[i]
                else:
                    new[(i, j)] = d[(i, j)] - scaled[i] * g(j, k)
        d = new
        g = lambda i, j, d=d: d[(i, j) if i <= j else (j, i)]
    return {ij: -v for ij, v in d.items()}

def solve_kernel(system_ref, rhs_ref, mine_ref, out_ref, a_ref, dinv_ref, sem):
    load = pltpu.make_async_copy(system_ref, a_ref, sem)
    load.start()
    lane = lax.broadcasted_iota(jnp.int32, (NI, KB), 1)
    b = rhs_ref[...]
    load.wait()
    pairs = [(i, j) for i in range(PANEL) for j in range(i, PANEL)]
    for p in range(KB // PANEL):
        k0 = p * PANEL
        rows = [a_ref[pl.ds((k0 + j) * NI, NI), :] for j in range(PANEL)]
        dinv = sweep_inverse({(i, j): lane_bcast(rows[i], k0 + j) for i, j in pairs}, PANEL)
        for n, ij in enumerate(pairs):
            dinv_ref[p, n] = dinv[ij]
        if p + 1 == KB // PANEL:
            break
        kept = [jnp.where(lane >= k0 + PANEL, r, 0.0) for r in rows]
        ws = [tree([dinv[(min(i, j), max(i, j))] * kept[j] for j in range(PANEL)]) for i in range(PANEL)]
        b = b - tree([lane_bcast(b, k0 + j) * ws[j] for j in range(PANEL)])
        first = (k0 + PANEL) * NI
        rest = a_ref[first:, :]
        count = KB * NI - first
        at = lax.broadcasted_iota(jnp.int32, (count, KB), 1)
        spread = jnp.take_along_axis(
            rest, k0 + jnp.bitwise_and(jnp.right_shift(at, 3), PANEL - 1), axis=1, mode="promise_in_bounds")
        item = jnp.bitwise_and(lax.broadcasted_iota(jnp.int32, (count, KB), 0), NI - 1)
        spread = jnp.where(jnp.bitwise_and(at, NI - 1) == item, spread, 0.0)
        h, m, l = split(spread)
        wh, wm, wl = split(jnp.concatenate(ws, axis=0))
        far = jnp.where(at < NI * PANEL, h.astype(F32), l.astype(F32)).astype(BF16)
        a_ref[first:, :] = rest - jnp.dot(
            jnp.concatenate([h, m, far], axis=1), jnp.concatenate([wh, wm, wh, wm, wl, wh], axis=0),
            preferred_element_type=F32)
    x = jnp.zeros((NI, KB), F32)
    for p in range(KB // PANEL - 1, -1, -1):
        k0 = p * PANEL
        bs = [lane_bcast(b, k0 + j) for j in range(PANEL)]
        dinv = {ij: dinv_ref[p, n] for n, ij in enumerate(pairs)}
        xs = [tree([dinv[(min(i, j), max(i, j))] * bs[j] for j in range(PANEL)]) for i in range(PANEL)]
        for j in range(PANEL):
            x = jnp.where(lane == k0 + j, xs[j], x)
        if p:
            b = b - tree([xs[j] * jnp.where(lane < k0, a_ref[pl.ds((k0 + j) * NI, NI), :], 0.0) for j in range(PANEL)])
    out_ref[...] = mine_ref[...] - x

def solve(system, rhs, mine):
    vmem = pl.BlockSpec(memory_space=pltpu.VMEM)
    return pl.pallas_call(
        solve_kernel,
        out_shape=jax.ShapeDtypeStruct((NI, KB), F32),
        in_specs=[pl.BlockSpec(memory_space=pl.ANY), vmem, vmem],
        out_specs=vmem,
        scratch_shapes=[
            pltpu.VMEM((KB * NI, KB), F32),
            pltpu.VMEM((KB // PANEL, PANEL * (PANEL + 1) // 2, NI, KB), F32),
            pltpu.SemaphoreType.DMA,
        ],
        compiler_params=pltpu.CompilerParams(vmem_limit_bytes=60 * 1024 * 1024),
        name="block_solve",
    )(system, rhs, mine)


def local(user_factors, item_factors, tile_user, tile_weight, tile_target):
    return solve(*normal_equations(
        user_factors.reshape(OWN, TILE, K), item_factors, tile_user[0], tile_weight[0, 0], tile_target[0, 0]))


def solution(mesh):
    return jax.shard_map(
        local,
        mesh=mesh,
        in_specs=(
            P("grp", "blk", None),
            P("blk", None),
            P("blk", "grp", None),
            P("blk", "grp", None, None, None),
            P("blk", "grp", None, None, None),
        ),
        out_specs=P(("blk", "grp"), None),
        check_vma=False,
    )
```

```python
import functools

import jax
import jax.numpy as jnp
from jax import lax
from jax.experimental import pallas as pl
from jax.experimental.pallas import tpu as pltpu
from jax.sharding import PartitionSpec as P

F32 = jnp.float32
BF16 = jnp.bfloat16
MESH = pl.DeviceIdType.MESH
K = 256
KB = 128
TILE = 128
NT = 8
PRIOR = 0.05
NI = 8
OWN = 16
ROWS = 32
NQ = TILE // ROWS
NCH = 2 * NQ
CU = NT * ROWS
NZ = 8
STEPS = 32000.0
TINY = 1e-18
BOTH_LAST = (((1,), (1,)), ((), ()))
BOTH_FIRST = (((0,), (0,)), ((), ()))


def gather_kernel(
    user_ref, tile_ref, item_ref, weight_ref, target_ref,
    system_ref, rhs_ref, mine_ref,
    pools, far_a, far_b, out_p, out_m, in_a, in_b, in_p, in_m, rights, zbufs,
    reqs, item, itemf, weight, target, wt_own, tt_own, wz, hacc, hsend, hin, dsend, din, hown, gsend, gin,
    gpart, gin1, gone, gin2, gtwo, gall, local_sem, send_sem, recv_sem,
):
    me_b, me_g = lax.axis_index("blk"), lax.axis_index("grp")
    y_lo, x, core = me_b // 8, lax.rem(me_b // 2, 4), lax.rem(me_b, 2)
    z, y_hi = me_g // 2, lax.rem(me_g, 2)
    own = y_lo * 2 + core
    across = (1 - y_lo) * 2 + core
    sibling = (me_b + 1 - 2 * core, me_g)
    y_peer = (lax.rem(me_b + 8, 16), me_g)
    x_at = [lax.rem(x + k, 4) for k in range(4)]
    x_peer = [(y_lo * 8 + x_at[k] * 2 + core, me_g) for k in range(4)]
    z_at = [lax.rem(z + k, NZ) for k in range(NZ)]
    z_peer = [(me_b, z_at[k] * 2 + y_hi) for k in range(NZ)]
    blk_at = [lax.rem(me_b + k, 16) for k in range(16)]
    grp_at = [lax.rem(me_g + k, 16) for k in range(16)]
    blk_peer = [(blk_at[k], me_g) for k in range(16)]
    grp_peer = [(me_b, grp_at[k]) for k in range(16)]
    partner = (me_b, me_g + 1 - 2 * y_hi)

    slots, sent = {}, []

    def slot(name):
        return slots.setdefault(name, len(slots))

    def send(name, src, dst, device):
        k = slot(name)
        copy = pltpu.make_async_remote_copy(
            src_ref=src, dst_ref=dst, send_sem=send_sem.at[k], recv_sem=recv_sem.at[k],
            device_id=device, device_id_type=MESH)
        copy.start()
        sent.append(copy)

    def arrived(name, dst):
        k = slot(name)
        pltpu.make_async_remote_copy(
            src_ref=dst, dst_ref=dst, send_sem=send_sem.at[k], recv_sem=recv_sem.at[k],
            device_id=sibling, device_id_type=MESH).wait_recv()

    def send_all(name, pairs):
        k = slot(name)
        for src, dst, device in pairs:
            copy = pltpu.make_async_remote_copy(
                src_ref=src, dst_ref=dst, send_sem=send_sem.at[k], recv_sem=recv_sem.at[k],
                device_id=device, device_id_type=MESH)
            copy.start()

    def all_of(name, whole):
        k = slot(name)
        return pltpu.make_async_remote_copy(
            src_ref=whole, dst_ref=whole, send_sem=send_sem.at[k], recv_sem=recv_sem.at[k],
            device_id=sibling, device_id_type=MESH)

    def all_arrived(name, whole):
        copy = all_of(name, whole)
        copy.wait_recv()
        sent.append(copy)

    locals_ = {}

    def fetch(name, src, dst):
        copy = pltpu.make_async_copy(src, dst, local_sem.at[len(locals_)])
        copy.start()
        locals_[name] = copy

    barrier = pltpu.get_barrier_semaphore()
    for k in range(1, 16):
        pl.semaphore_signal(barrier, inc=1, device_id=blk_peer[k], device_id_type=MESH)
        pl.semaphore_signal(barrier, inc=1, device_id=grp_peer[k], device_id_type=MESH)
    for c in range(NCH):
        rows, cols = (c % NQ) * ROWS, (c // NQ) * KB
        fetch(("pool", c), user_ref.at[:, pl.ds(rows, ROWS), pl.ds(cols, KB)], pools[c].at[own])
    fetch("tile", tile_ref, reqs.at[x])
    fetch("weight", weight_ref, weight)
    fetch("target", target_ref, target)
    fetch("item", item_ref, item)

    for name in [("pool", c) for c in range(NCH)] + ["tile"]:
        locals_[name].wait()
    pl.semaphore_wait(barrier, 30)

    def send_chunk(c):
        send(("y", c), pools[c].at[own], pools[c].at[own], y_peer)
        send(("s", c), pools[c].at[own], pools[c].at[own], sibling)

    def forward_chunk(c):
        arrived(("y", c), pools[c].at[across])
        send(("f", c), pools[c].at[across], pools[c].at[across], sibling)

    def finish_pool(c):
        other = y_lo * 2 + 1 - core
        diagonal = (1 - y_lo) * 2 + 1 - core
        arrived(("s", c), pools[c].at[other])
        arrived(("f", c), pools[c].at[diagonal])

    def wanted(k, j):
        return reqs[x_at[k], 0, j]

    def column(t):
        return jnp.bitwise_and(jnp.right_shift(t, 5), 3)

    def pick(c, t):
        owner = jnp.right_shift(t, 7) * 2 + jnp.bitwise_and(jnp.right_shift(t, 4), 1)
        return pools[c][owner, jnp.bitwise_and(t, 15)]

    half = ROWS // 2

    def x_pack(c):
        for j in range(NT):
            v = pick(c, wanted(2, j))
            far_a[c][j] = v[:half]
            far_b[c][j] = v[half:]
        send(("xa", c), far_a[c], in_a[c], x_peer[1])
        send(("xb", c), far_b[c], in_b[c], x_peer[3])
        for j in range(NT):
            out_p[c][1, j] = pick(c, wanted(1, j))[half:]
            out_m[c][0, j] = pick(c, wanted(3, j))[:half]
        send(("p1", c), out_p[c].at[1], in_m[c].at[1], x_peer[1])
        send(("m0", c), out_m[c].at[0], in_p[c].at[0], x_peer[3])

    def x_merge(c):
        arrived(("xa", c), in_a[c])
        for j in range(NT):
            t = wanted(1, j)
            out_p[c][0, j] = jnp.where(column(t) == x, pick(c, t)[:half], in_a[c][j])
        send(("p0", c), out_p[c].at[0], in_m[c].at[0], x_peer[1])
        arrived(("xb", c), in_b[c])
        for j in range(NT):
            t = wanted(3, j)
            out_m[c][1, j] = jnp.where(column(t) == x, pick(c, t)[half:], in_b[c][j])
        send(("m1", c), out_m[c].at[1], in_p[c].at[1], x_peer[3])

    def x_final(c):
        arrived(("p1", c), in_m[c].at[1])
        arrived(("m0", c), in_p[c].at[0])
        arrived(("p0", c), in_m[c].at[0])
        arrived(("m1", c), in_p[c].at[1])
        for j in range(NT):
            t = wanted(0, j)
            away = jnp.bitwise_and(column(t) - x + 4, 3)
            mine = pick(c, t)
            first = jnp.where(away == 0, mine[:half], jnp.where(away == 1, in_p[c][0, j], in_m[c][0, j]))
            second = jnp.where(away == 0, mine[half:], jnp.where(away == 3, in_m[c][1, j], in_p[c][1, j]))
            put(c, j, first, second)

    def x_pack_direct(c):
        for j in range(NT):
            v = pick(c, wanted(2, j))
            far_a[c][j] = v[:half]
            far_b[c][j] = v[half:]
        send(("xa", c), far_a[c], in_a[c], x_peer[2])
        send(("xb", c), far_b[c], in_b[c], x_peer[2])
        for j in range(NT):
            v = pick(c, wanted(1, j))
            out_p[c][0, j] = v[:half]
            out_p[c][1, j] = v[half:]
            v = pick(c, wanted(3, j))
            out_m[c][0, j] = v[:half]
            out_m[c][1, j] = v[half:]
        send(("p0", c), out_p[c], in_m[c], x_peer[1])
        send(("m0", c), out_m[c], in_p[c], x_peer[3])

    def x_final_direct(c):
        arrived(("p0", c), in_m[c])
        arrived(("m0", c), in_p[c])
        arrived(("xa", c), in_a[c])
        arrived(("xb", c), in_b[c])
        for j in range(NT):
            t = wanted(0, j)
            away = jnp.bitwise_and(column(t) - x + 4, 3)
            mine = pick(c, t)
            parts = []
            for p, far in ((0, in_a[c][j]), (1, in_b[c][j])):
                near = jnp.where(away == 1, in_p[c][p, j], in_m[c][p, j])
                parts.append(jnp.where(away == 0, mine[p * half:(p + 1) * half], jnp.where(away == 2, far, near)))
            put(c, j, *parts)

    def put(c, j, first, second):
        if c < NQ:
            zbufs[c][z, j, :half] = first
            zbufs[c][z, j, half:] = second
        else:
            rights[c - NQ][j, :half] = first
            rights[c - NQ][j, half:] = second

    def slots_of(q, source, part):
        return zbufs[q].at[source, pl.ds(part * (NT // 2), NT // 2)]

    def z_start(q):
        for first in (0, 1):
            for side, part, peer in (("zr", first, z_peer[1]), ("zl", 1 - first, z_peer[7])):
                mine = slots_of(q, z, part)
                send((side, q, 1, part), mine, mine, peer)

    def z_hop(q, h):
        for first in (0, 1) if h < 4 else (0,):
            for side, part, source, peer in (
                ("zr", first, z_at[NZ - h], z_peer[1]), ("zl", 1 - first, z_at[h], z_peer[7])):
                here = slots_of(q, source, part)
                arrived((side, q, h, part), here)
                if h < 3 or (h == 3 and first == 0):
                    send((side, q, h + 1, part), here, here, peer)

    def transposed(ref, out):
        span = TILE // ROWS
        for q in range(NQ):
            for p in range(NT // span):
                block = ref[p * span:(p + 1) * span, q * ROWS:(q + 1) * ROWS, :].reshape(TILE, TILE)
                out[:, :, pl.ds((q * (NT // span) + p) * TILE, TILE)] = block.T.reshape(NZ, 16, TILE)

    def send_weights():
        locals_["weight"].wait()
        transposed(weight, wt_own)
        send_all("w", [(wt_own.at[z_at[k]], wz.at[z], z_peer[k]) for k in range(1, NZ)])
        wz[z] = wt_own[z]

    def weights_arrived():
        all_arrived("w", wz.at[pl.ds(0, NZ - 1)])

    def gram_start():
        left = jnp.zeros((KB, KB), F32)
        right = jnp.zeros((KB, KB), F32)
        for q in range(NQ):
            a = pools[q][own].reshape(OWN * ROWS, KB)
            b = pools[NQ + q][own].reshape(OWN * ROWS, KB)
            left += lax.dot_general(a, a, BOTH_FIRST, preferred_element_type=F32)
            right += lax.dot_general(a, b, BOTH_FIRST, preferred_element_type=F32)
        gpart[:, 0] = left.reshape(16, 8, KB)
        gpart[:, 1] = right.reshape(16, 8, KB)
        send_all("g1", [(gpart.at[blk_at[k]], gin1.at[me_b], blk_peer[k]) for k in range(1, 16)])
        gin1[me_b] = gpart[me_b]

    def gram_second():
        all_arrived("g1", gin1.at[pl.ds(0, 15)])
        gone[...] = jnp.sum(gin1[...], axis=0)
        send_all("g2", [(gone, gin2.at[me_g], grp_peer[k]) for k in range(1, 16)])
        gin2[me_g] = gone[...]

    def gram_third():
        all_arrived("g2", gin2.at[pl.ds(0, 15)])
        gtwo[...] = jnp.sum(gin2[...], axis=0)
        send_all("g3", [(gtwo, gall.at[me_b], blk_peer[k]) for k in range(1, 16)])
        gall[me_b] = gtwo[...]

    def gram_last():
        all_arrived("g3", gall.at[pl.ds(0, 15)])

    GROUP = 4

    def hess_piece(q, sources, start=False, last=False):
        users = [zbufs[q][s].reshape(CU, KB) for s in sources]
        users_t = jnp.concatenate(
            [u[p * KB:(p + 1) * KB].T for u in users for p in range(CU // KB)], axis=1)
        width = CU * len(sources)
        users_t = users_t.reshape(KB // 16, 16, width)
        users = jnp.concatenate(users, axis=0)
        scale = jnp.concatenate([wz[s, :, pl.ds(q * CU, CU)].astype(F32) for s in sources], axis=1)
        theirs = jnp.where(y_hi == 0, scale[8:], scale[:8])
        ours = jnp.where(y_hi == 0, scale[:8], scale[8:])
        scale = jnp.concatenate([theirs, ours], axis=0)
        for i0 in range(0, 16, GROUP):
            lhs = []
            for i in range(i0, i0 + GROUP):
                row = jnp.broadcast_to(scale[i:i + 1], (16, width)).astype(BF16)
                lhs.append((row[None] * users_t).reshape(KB, width))
            part = jnp.dot(jnp.concatenate(lhs, axis=0), users, preferred_element_type=F32)
            part = part.reshape(GROUP, KB, KB)
            if start:
                hacc[i0:i0 + GROUP] = part
            else:
                hacc[i0:i0 + GROUP] += part
            if last and i0 < NI:
                for i in range(i0, i0 + GROUP, 2):
                    fold(i)

    def row_col():
        return (lax.broadcasted_iota(jnp.int32, (KB, KB), 0), lax.broadcasted_iota(jnp.int32, (KB, KB), 1))

    def diagonal(square):
        row, col = row_col()
        kept = jnp.where(row == col, square, 0.0)
        return jnp.sum(kept, axis=0, keepdims=True), jnp.sum(kept, axis=1, keepdims=True)

    def inverse_root(d):
        root = jnp.sqrt(d)
        return jnp.where(root > TINY, 1.0 / jnp.maximum(root, TINY), 0.0)

    def fold(i):
        row, col = row_col()
        upper, lower = hacc[i], hacc[i + 1]
        upper_row, upper_col = diagonal(upper)
        lower_row, lower_col = diagonal(lower)
        square = jnp.where(row <= col, upper, lower)
        by_col = jnp.where(row <= col, inverse_root(upper_col), inverse_root(lower_col))
        by_row = jnp.where(row <= col, inverse_root(upper_row), inverse_root(lower_row))
        coded = jnp.round(square * by_col * by_row * STEPS)
        coded = jnp.minimum(jnp.maximum(coded, -32767.0), 32767.0)
        hsend[i // 2] = coded.astype(jnp.int32).astype(jnp.int16)
        first = lax.broadcasted_iota(jnp.int32, (8, KB), 0) == 0
        dsend[i // 2] = jnp.where(first, upper_row, lower_row)
        send(("h", i), hsend.at[i // 2], hin.at[i // 2], partner)
        send(("d", i), dsend.at[i // 2], din.at[i // 2], partner)

    def own_systems():
        prior = PRIOR * gall[:, 0].reshape(KB, KB)
        for i in range(NI):
            h = hacc[NI + i]
            hown[i] = 0.5 * (h + h.T) + prior

    def join_systems():
        row, col = row_col()
        for i in range(0, NI, 2):
            arrived(("d", i), din.at[i // 2])
            upper_row, lower_row = din[i // 2, 0:1], din[i // 2, 1:2]
            upper_root, lower_root = jnp.sqrt(upper_row), jnp.sqrt(lower_row)
            as_col = lambda r: jnp.sum(jnp.where(row == col, r, 0.0), axis=1, keepdims=True)
            by_col = jnp.where(row <= col, as_col(upper_root), as_col(lower_root))
            by_row = jnp.where(row <= col, upper_root, lower_root)
            scale = by_col * by_row * (1.0 / STEPS)
            arrived(("h", i), hin.at[i // 2])
            square = hin[i // 2].astype(jnp.int32).astype(F32) * scale
            turned = square.T
            first = jnp.where(row < col, square, jnp.where(row == col, upper_row, turned))
            second = jnp.where(row > col, square, jnp.where(row == col, lower_row, turned))
            system_ref[pl.ds(i, KB, stride=NI), :] = hown[i] + first
            system_ref[pl.ds(i + 1, KB, stride=NI), :] = hown[i + 1] + second

    def drain():
        for copy in sent:
            copy.wait_send()
        sent.clear()

    def grad_start():
        total = jnp.zeros((TILE, KB), F32)
        items = item[...]
        for q in range(NQ):
            left = zbufs[q][z].reshape(CU, KB)
            right = rights[q][...].reshape(CU, KB)
            pred = lax.dot_general(items[:, :KB], left, BOTH_LAST, preferred_element_type=F32)
            pred += lax.dot_general(items[:, KB:], right, BOTH_LAST, preferred_element_type=F32)
            w = wt_own[:, :, pl.ds(q * CU, CU)].reshape(TILE, CU).astype(F32)
            t = tt_own[:, :, pl.ds(q * CU, CU)].reshape(TILE, CU).astype(F32)
            resid = (w * (pred - t)).astype(BF16)
            total += jnp.dot(resid, left, preferred_element_type=F32)
        gsend[...] = total.reshape(16, NI, KB)
        send_all("gr", [(gsend.at[grp_at[k]], gin.at[me_g], grp_peer[k]) for k in range(1, 16)])
        gin[me_g] = gsend[me_g]

    def rhs_start():
        itemf[...] = item[...].astype(F32)
        mine = itemf[pl.ds(me_g * NI, NI), :]
        mine_ref[...] = mine[:, :KB]
        exact = lax.Precision.HIGHEST
        rhs_ref[...] = PRIOR * (
            lax.dot_general(mine[:, :KB], gall[:, 0].reshape(KB, KB), BOTH_LAST,
                            precision=exact, preferred_element_type=F32)
            + lax.dot_general(mine[:, KB:], gall[:, 1].reshape(KB, KB), BOTH_LAST,
                              precision=exact, preferred_element_type=F32))

    def grad_last():
        all_arrived("gr", gin.at[pl.ds(0, 15)])
        rhs_ref[...] += jnp.sum(gin[...], axis=0)

    def target_ready():
        locals_["target"].wait()
        transposed(target, tt_own)
        locals_["item"].wait()

    def send_requests():
        for k in range(1, 4):
            send(("rq", k), reqs.at[x], reqs.at[x], x_peer[k])

    def requests_arrived():
        for k in range(1, 4):
            arrived(("rq", k), reqs.at[x_at[4 - k]])

    send_requests()
    send_chunk(0)
    send_chunk(1)
    send_chunk(2)
    send_weights()
    gram_start()
    target_ready()
    forward_chunk(0)
    send_chunk(3)
    requests_arrived()
    finish_pool(0)
    x_pack_direct(0)
    forward_chunk(1)
    send_chunk(4)
    weights_arrived()
    finish_pool(1)
    x_pack_direct(1)
    forward_chunk(2)
    send_chunk(5)
    gram_second()
    finish_pool(2)
    x_pack_direct(2)
    forward_chunk(3)
    send_chunk(6)
    x_final_direct(0)
    z_start(0)
    x_final_direct(1)
    z_start(1)
    finish_pool(3)
    x_pack_direct(3)
    forward_chunk(4)
    send_chunk(7)
    z_hop(0, 1)
    hess_piece(0, (z_at[7], z_at[1]), start=True)
    finish_pool(4)
    x_pack(4)
    forward_chunk(5)
    x_final_direct(2)
    z_start(2)
    z_hop(1, 1)
    hess_piece(1, (z_at[7], z_at[1]))
    z_hop(0, 2)
    hess_piece(0, (z_at[6], z_at[2]))
    finish_pool(5)
    x_pack(5)
    forward_chunk(6)
    x_merge(4)
    x_final_direct(3)
    z_start(3)
    z_hop(2, 1)
    hess_piece(2, (z_at[7], z_at[1]))
    gram_third()
    finish_pool(6)
    x_pack(6)
    forward_chunk(7)
    x_merge(5)
    z_hop(1, 2)
    hess_piece(1, (z_at[6], z_at[2]))
    x_final(4)
    z_hop(0, 3)
    hess_piece(0, (z_at[5], z_at[3]))
    z_hop(3, 1)
    finish_pool(7)
    x_pack(7)
    x_merge(6)
    hess_piece(3, (z_at[7], z_at[1]))
    z_hop(2, 2)
    hess_piece(2, (z_at[6], z_at[2]))
    x_final(5)
    z_hop(1, 3)
    hess_piece(1, (z_at[5], z_at[3]))
    x_merge(7)
    z_hop(0, 4)
    hess_piece(0, (z, z_at[4]))
    x_final(6)
    z_hop(3, 2)
    hess_piece(3, (z_at[6], z_at[2]))
    z_hop(2, 3)
    x_final(7)
    grad_start()
    z_hop(1, 4)
    hess_piece(2, (z_at[5], z_at[3]))
    z_hop(3, 3)
    gram_last()
    rhs_start()
    hess_piece(1, (z, z_at[4]))
    z_hop(2, 4)
    hess_piece(3, (z_at[5], z_at[3]))
    hess_piece(2, (z, z_at[4]))
    z_hop(3, 4)
    hess_piece(3, (z, z_at[4]), last=True)
    own_systems()
    drain()
    grad_last()
    join_systems()
    for copy in sent:
        copy.wait_send()
    assert len(slots) <= NSEM, len(slots)


NSEM = 240


def normal_equations(user_factors, item_factors, tile_user, tile_weight, tile_target):
    vm = pltpu.VMEM
    chunk = (NT, ROWS // 2, KB)
    both = (2,) + chunk
    return pl.pallas_call(
        gather_kernel,
        out_shape=(
            jax.ShapeDtypeStruct((KB * NI, KB), F32),
            jax.ShapeDtypeStruct((NI, KB), F32),
            jax.ShapeDtypeStruct((NI, KB), F32),
        ),
        in_specs=[pl.BlockSpec(memory_space=pl.ANY)] * 5,
        out_specs=(pl.BlockSpec(memory_space=pltpu.VMEM),) * 3,
        scratch_shapes=[
            [vm((4, OWN, ROWS, KB), BF16)] * NCH,
            [vm(chunk, BF16)] * NCH,
            [vm(chunk, BF16)] * NCH,
            [vm(both, BF16)] * NCH,
            [vm(both, BF16)] * NCH,
            [vm(chunk, BF16)] * NCH,
            [vm(chunk, BF16)] * NCH,
            [vm(both, BF16)] * NCH,
            [vm(both, BF16)] * NCH,
            [vm((NT, ROWS, KB), BF16)] * NQ,
            [vm((NZ, NT, ROWS, KB), BF16)] * NQ,
            pltpu.SMEM((4, 1, NT), jnp.int32),
            vm((TILE, K), BF16),
            vm((TILE, K), F32),
            vm((NT, TILE, TILE), BF16),
            vm((NT, TILE, TILE), BF16),
            vm((NZ, 16, NT * TILE), BF16),
            vm((NZ, 16, NT * TILE), BF16),
            vm((NZ, 16, NT * TILE), BF16),
            vm((16, KB, KB), F32),
            vm((NI // 2, KB, KB), jnp.int16),
            vm((NI // 2, KB, KB), jnp.int16),
            vm((NI // 2, 8, KB), F32),
            vm((NI // 2, 8, KB), F32),
            vm((NI, KB, KB), F32),
            vm((16, NI, KB), F32),
            vm((16, NI, KB), F32),
            vm((16, 2, 8, KB), F32),
            vm((16, 2, 8, KB), F32),
            vm((2, 8, KB), F32),
            vm((16, 2, 8, KB), F32),
            vm((2, 8, KB), F32),
            vm((16, 2, 8, KB), F32),
            pltpu.SemaphoreType.DMA((NCH + 4,)),
            pltpu.SemaphoreType.DMA((NSEM,)),
            pltpu.SemaphoreType.DMA((NSEM,)),
        ],
        compiler_params=pltpu.CompilerParams(
            collective_id=0, has_side_effects=True, vmem_limit_bytes=60 * 1024 * 1024),
        name="normal_equations",
    )(user_factors, tile_user, item_factors, tile_weight, tile_target)


PANEL = 8


def lane_bcast(v, lane):
    return jnp.broadcast_to(v[:, lane:lane+1], v.shape)

def tree(xs):
    while len(xs) > 1:
        xs = [xs[i] + xs[i+1] if i+1 < len(xs) else xs[i] for i in range(0, len(xs), 2)]
    return xs[0]

def split(v):
    h = v.astype(BF16)
    rest = v - h.astype(F32)
    m = rest.astype(BF16)
    return h, m, (rest - m.astype(F32)).astype(BF16)


def sweep_inverse(d, n):
    g = lambda i, j: d[(i, j) if i <= j else (j, i)]
    for k in range(n):
        inv = 1.0 / g(k, k)
        scaled = {i: g(i, k) * inv for i in range(n) if i != k}
        new = {}
        for i in range(n):
            for j in range(i, n):
                if i == k and j == k:
                    new[(i, j)] = -inv
                elif i == k:
                    new[(i, j)] = scaled[j]
                elif j == k:
                    new[(i, j)] = scaled[i]
                else:
                    new[(i, j)] = d[(i, j)] - scaled[i] * g(j, k)
        d = new
        g = lambda i, j, d=d: d[(i, j) if i <= j else (j, i)]
    return {ij: -v for ij, v in d.items()}

def solve_kernel(system_ref, rhs_ref, mine_ref, out_ref, a_ref, dinv_ref, sem):
    load = pltpu.make_async_copy(system_ref, a_ref, sem)
    load.start()
    lane = lax.broadcasted_iota(jnp.int32, (NI, KB), 1)
    b = rhs_ref[...]
    load.wait()
    pairs = [(i, j) for i in range(PANEL) for j in range(i, PANEL)]
    for p in range(KB // PANEL):
        k0 = p * PANEL
        rows = [a_ref[pl.ds((k0 + j) * NI, NI), :] for j in range(PANEL)]
        dinv = sweep_inverse({(i, j): lane_bcast(rows[i], k0 + j) for i, j in pairs}, PANEL)
        for n, ij in enumerate(pairs):
            dinv_ref[p, n] = dinv[ij]
        if p + 1 == KB // PANEL:
            break
        kept = [jnp.where(lane >= k0 + PANEL, r, 0.0) for r in rows]
        ws = [tree([dinv[(min(i, j), max(i, j))] * kept[j] for j in range(PANEL)]) for i in range(PANEL)]
        b = b - tree([lane_bcast(b, k0 + j) * ws[j] for j in range(PANEL)])
        first = (k0 + PANEL) * NI
        rest = a_ref[first:, :]
        count = KB * NI - first
        at = lax.broadcasted_iota(jnp.int32, (count, KB), 1)
        spread = jnp.take_along_axis(
            rest, k0 + jnp.bitwise_and(jnp.right_shift(at, 3), PANEL - 1), axis=1, mode="promise_in_bounds")
        item = jnp.bitwise_and(lax.broadcasted_iota(jnp.int32, (count, KB), 0), NI - 1)
        spread = jnp.where(jnp.bitwise_and(at, NI - 1) == item, spread, 0.0)
        h, m, l = split(spread)
        wh, wm, wl = split(jnp.concatenate(ws, axis=0))
        far = jnp.where(at < NI * PANEL, h.astype(F32), l.astype(F32)).astype(BF16)
        a_ref[first:, :] = rest - jnp.dot(
            jnp.concatenate([h, m, far], axis=1), jnp.concatenate([wh, wm, wh, wm, wl, wh], axis=0),
            preferred_element_type=F32)
    x = jnp.zeros((NI, KB), F32)
    for p in range(KB // PANEL - 1, -1, -1):
        k0 = p * PANEL
        bs = [lane_bcast(b, k0 + j) for j in range(PANEL)]
        dinv = {ij: dinv_ref[p, n] for n, ij in enumerate(pairs)}
        xs = [tree([dinv[(min(i, j), max(i, j))] * bs[j] for j in range(PANEL)]) for i in range(PANEL)]
        for j in range(PANEL):
            x = jnp.where(lane == k0 + j, xs[j], x)
        if p:
            b = b - tree([xs[j] * jnp.where(lane < k0, a_ref[pl.ds((k0 + j) * NI, NI), :], 0.0) for j in range(PANEL)])
    out_ref[...] = mine_ref[...] - x

def solve(system, rhs, mine):
    vmem = pl.BlockSpec(memory_space=pltpu.VMEM)
    return pl.pallas_call(
        solve_kernel,
        out_shape=jax.ShapeDtypeStruct((NI, KB), F32),
        in_specs=[pl.BlockSpec(memory_space=pl.ANY), vmem, vmem],
        out_specs=vmem,
        scratch_shapes=[
            pltpu.VMEM((KB * NI, KB), F32),
            pltpu.VMEM((KB // PANEL, PANEL * (PANEL + 1) // 2, NI, KB), F32),
            pltpu.SemaphoreType.DMA,
        ],
        compiler_params=pltpu.CompilerParams(vmem_limit_bytes=60 * 1024 * 1024),
        name="block_solve",
    )(system, rhs, mine)


def local(user_factors, item_factors, tile_user, tile_weight, tile_target):
    return solve(*normal_equations(
        user_factors.reshape(OWN, TILE, K), item_factors, tile_user[0], tile_weight[0, 0], tile_target[0, 0]))


def solution(mesh):
    return jax.shard_map(
        local,
        mesh=mesh,
        in_specs=(
            P("grp", "blk", None),
            P("blk", None),
            P("blk", "grp", None),
            P("blk", "grp", None, None, None),
            P("blk", "grp", None, None, None),
        ),
        out_specs=P(("blk", "grp"), None),
        check_vma=False,
    )
```

```python
import functools

import jax
import jax.numpy as jnp
from jax import lax
from jax.experimental import pallas as pl
from jax.experimental.pallas import tpu as pltpu
from jax.sharding import PartitionSpec as P

F32 = jnp.float32
BF16 = jnp.bfloat16
MESH = pl.DeviceIdType.MESH
K = 256
KB = 128
TILE = 128
NT = 8
PRIOR = 0.05
NI = 8
OWN = 16
ROWS = 32
NQ = TILE // ROWS
NCH = 2 * NQ
CU = NT * ROWS
NZ = 8
PANEL = 8
STEPS = 32000.0
TINY = 1e-18
BOTH_LAST = (((1,), (1,)), ((), ()))
BOTH_FIRST = (((0,), (0,)), ((), ()))


def gather_kernel(
    user_ref, tile_ref, item_ref, weight_ref, target_ref,
    out_ref,
    pools, far_a, far_b, out_p, out_m, in_a, in_b, in_p, in_m, rights, zbufs,
    reqs, item, itemf, weight, target, wt_own, tt_own, wz, hacc, hsend, hin, dsend, din, hown, gsend, gin,
    gpart, gin1, gone, gin2, gtwo, gall, system_ref, rhs_ref, mine_ref, dinv_ref, local_sem, send_sem, recv_sem,
):
    me_b, me_g = lax.axis_index("blk"), lax.axis_index("grp")
    y_lo, x, core = me_b // 8, lax.rem(me_b // 2, 4), lax.rem(me_b, 2)
    z, y_hi = me_g // 2, lax.rem(me_g, 2)
    own = y_lo * 2 + core
    across = (1 - y_lo) * 2 + core
    sibling = (me_b + 1 - 2 * core, me_g)
    y_peer = (lax.rem(me_b + 8, 16), me_g)
    x_at = [lax.rem(x + k, 4) for k in range(4)]
    x_peer = [(y_lo * 8 + x_at[k] * 2 + core, me_g) for k in range(4)]
    z_at = [lax.rem(z + k, NZ) for k in range(NZ)]
    z_peer = [(me_b, z_at[k] * 2 + y_hi) for k in range(NZ)]
    blk_at = [lax.rem(me_b + k, 16) for k in range(16)]
    grp_at = [lax.rem(me_g + k, 16) for k in range(16)]
    blk_peer = [(blk_at[k], me_g) for k in range(16)]
    grp_peer = [(me_b, grp_at[k]) for k in range(16)]
    partner = (me_b, me_g + 1 - 2 * y_hi)

    slots, sent = {}, []

    def slot(name):
        return slots.setdefault(name, len(slots))

    def send(name, src, dst, device):
        k = slot(name)
        copy = pltpu.make_async_remote_copy(
            src_ref=src, dst_ref=dst, send_sem=send_sem.at[k], recv_sem=recv_sem.at[k],
            device_id=device, device_id_type=MESH)
        copy.start()
        sent.append(copy)

    def arrived(name, dst):
        k = slot(name)
        pltpu.make_async_remote_copy(
            src_ref=dst, dst_ref=dst, send_sem=send_sem.at[k], recv_sem=recv_sem.at[k],
            device_id=sibling, device_id_type=MESH).wait_recv()

    def send_all(name, pairs):
        k = slot(name)
        for src, dst, device in pairs:
            copy = pltpu.make_async_remote_copy(
                src_ref=src, dst_ref=dst, send_sem=send_sem.at[k], recv_sem=recv_sem.at[k],
                device_id=device, device_id_type=MESH)
            copy.start()

    def all_of(name, whole):
        k = slot(name)
        return pltpu.make_async_remote_copy(
            src_ref=whole, dst_ref=whole, send_sem=send_sem.at[k], recv_sem=recv_sem.at[k],
            device_id=sibling, device_id_type=MESH)

    def all_arrived(name, whole):
        copy = all_of(name, whole)
        copy.wait_recv()
        sent.append(copy)

    locals_ = {}

    def fetch(name, src, dst):
        copy = pltpu.make_async_copy(src, dst, local_sem.at[len(locals_)])
        copy.start()
        locals_[name] = copy

    fetch("tile", tile_ref, reqs.at[x])
    for c in range(NCH):
        rows, cols = (c % NQ) * ROWS, (c // NQ) * KB
        fetch(("pool", c), user_ref.at[:, pl.ds(rows, ROWS), pl.ds(cols, KB)], pools[c].at[own])
    fetch("weight", weight_ref, weight)
    fetch("target", target_ref, target)
    fetch("item", item_ref, item)

    barrier = pltpu.get_barrier_semaphore()
    for k in range(1, 16):
        pl.semaphore_signal(barrier, inc=1, device_id=blk_peer[k], device_id_type=MESH)
        pl.semaphore_signal(barrier, inc=1, device_id=grp_peer[k], device_id_type=MESH)

    def fetched(name):
        if name in locals_:
            locals_.pop(name).wait()

    pl.semaphore_wait(barrier, 30)

    def send_chunk(c):
        fetched(("pool", c))
        send(("y", c), pools[c].at[own], pools[c].at[own], y_peer)
        send(("s", c), pools[c].at[own], pools[c].at[own], sibling)

    def forward_chunk(c):
        arrived(("y", c), pools[c].at[across])
        send(("f", c), pools[c].at[across], pools[c].at[across], sibling)

    def finish_pool(c):
        other = y_lo * 2 + 1 - core
        diagonal = (1 - y_lo) * 2 + 1 - core
        arrived(("s", c), pools[c].at[other])
        arrived(("f", c), pools[c].at[diagonal])

    def wanted(k, j):
        return reqs[x_at[k], 0, j]

    def column(t):
        return jnp.bitwise_and(jnp.right_shift(t, 5), 3)

    def pick(c, t):
        owner = jnp.right_shift(t, 7) * 2 + jnp.bitwise_and(jnp.right_shift(t, 4), 1)
        return pools[c][owner, jnp.bitwise_and(t, 15)]

    half = ROWS // 2

    def x_pack(c):
        for j in range(NT):
            v = pick(c, wanted(2, j))
            far_a[c][j] = v[:half]
            far_b[c][j] = v[half:]
        send(("xa", c), far_a[c], in_a[c], x_peer[2])
        send(("xb", c), far_b[c], in_b[c], x_peer[2])
        for j in range(NT):
            v = pick(c, wanted(1, j))
            out_p[c][0, j] = v[:half]
            out_p[c][1, j] = v[half:]
            v = pick(c, wanted(3, j))
            out_m[c][0, j] = v[:half]
            out_m[c][1, j] = v[half:]
        send(("p0", c), out_p[c], in_m[c], x_peer[1])
        send(("m0", c), out_m[c], in_p[c], x_peer[3])

    def x_final(c):
        arrived(("p0", c), in_m[c])
        arrived(("m0", c), in_p[c])
        arrived(("xa", c), in_a[c])
        arrived(("xb", c), in_b[c])
        for j in range(NT):
            t = wanted(0, j)
            away = jnp.bitwise_and(column(t) - x + 4, 3)
            mine = pick(c, t)
            parts = []
            for p, far in ((0, in_a[c][j]), (1, in_b[c][j])):
                near = jnp.where(away == 1, in_p[c][p, j], in_m[c][p, j])
                parts.append(jnp.where(away == 0, mine[p * half:(p + 1) * half], jnp.where(away == 2, far, near)))
            put(c, j, *parts)

    def put(c, j, first, second):
        if c < NQ:
            zbufs[c][z, j, :half] = first
            zbufs[c][z, j, half:] = second
        else:
            rights[c - NQ][j, :half] = first
            rights[c - NQ][j, half:] = second

    def slots_of(q, source, part):
        return zbufs[q].at[source, pl.ds(part * (NT // 2), NT // 2)]

    def z_start(q):
        for first in (0, 1):
            for side, part, peer in (("zr", first, z_peer[1]), ("zl", 1 - first, z_peer[7])):
                mine = slots_of(q, z, part)
                send((side, q, 1, part), mine, mine, peer)

    def z_hop(q, h):
        for first in (0, 1) if h < 4 else (0,):
            for side, part, source, peer in (
                ("zr", first, z_at[NZ - h], z_peer[1]), ("zl", 1 - first, z_at[h], z_peer[7])):
                here = slots_of(q, source, part)
                arrived((side, q, h, part), here)
                if h < 3 or (h == 3 and first == 0):
                    send((side, q, h + 1, part), here, here, peer)

    def transposed(ref, out):
        span = TILE // ROWS
        for q in range(NQ):
            for p in range(NT // span):
                block = ref[p * span:(p + 1) * span, q * ROWS:(q + 1) * ROWS, :].reshape(TILE, TILE)
                out[:, :, pl.ds((q * (NT // span) + p) * TILE, TILE)] = block.T.reshape(NZ, 16, TILE)

    def send_weights():
        fetched("weight")
        transposed(weight, wt_own)
        send_all("w", [(wt_own.at[z_at[k]], wz.at[z], z_peer[k]) for k in range(1, NZ)])
        wz[z] = wt_own[z]

    def weights_arrived():
        all_arrived("w", wz.at[pl.ds(0, NZ - 1)])

    def gram_start():
        for c in range(NCH):
            fetched(("pool", c))
        left = jnp.zeros((KB, KB), F32)
        right = jnp.zeros((KB, KB), F32)
        for q in range(NQ):
            a = pools[q][own].reshape(OWN * ROWS, KB)
            b = pools[NQ + q][own].reshape(OWN * ROWS, KB)
            left += lax.dot_general(a, a, BOTH_FIRST, preferred_element_type=F32)
            right += lax.dot_general(a, b, BOTH_FIRST, preferred_element_type=F32)
        gpart[:, 0] = left.reshape(16, 8, KB)
        gpart[:, 1] = right.reshape(16, 8, KB)
        send_all("g1", [(gpart.at[blk_at[k]], gin1.at[me_b], blk_peer[k]) for k in range(1, 16)])
        gin1[me_b] = gpart[me_b]

    def gram_second():
        all_arrived("g1", gin1.at[pl.ds(0, 15)])
        gone[...] = jnp.sum(gin1[...], axis=0)
        send_all("g2", [(gone, gin2.at[me_g], grp_peer[k]) for k in range(1, 16)])
        gin2[me_g] = gone[...]

    def gram_third():
        all_arrived("g2", gin2.at[pl.ds(0, 15)])
        gtwo[...] = jnp.sum(gin2[...], axis=0)
        send_all("g3", [(gtwo, gall.at[me_b], blk_peer[k]) for k in range(1, 16)])
        gall[me_b] = gtwo[...]

    def gram_last():
        all_arrived("g3", gall.at[pl.ds(0, 15)])

    GROUP = 4

    def hess_piece(q, sources, start=False, last=False):
        users = [zbufs[q][s].reshape(CU, KB) for s in sources]
        users_t = jnp.concatenate(
            [u[p * KB:(p + 1) * KB].T for u in users for p in range(CU // KB)], axis=1)
        width = CU * len(sources)
        users_t = users_t.reshape(KB // 16, 16, width)
        users = jnp.concatenate(users, axis=0)
        scale = jnp.concatenate([wz[s, :, pl.ds(q * CU, CU)].astype(F32) for s in sources], axis=1)
        theirs = jnp.where(y_hi == 0, scale[8:], scale[:8])
        ours = jnp.where(y_hi == 0, scale[:8], scale[8:])
        scale = jnp.concatenate([theirs, ours], axis=0)
        for i0 in range(0, 16, GROUP):
            lhs = []
            for i in range(i0, i0 + GROUP):
                row = jnp.broadcast_to(scale[i:i + 1], (16, width)).astype(BF16)
                lhs.append((row[None] * users_t).reshape(KB, width))
            part = jnp.dot(jnp.concatenate(lhs, axis=0), users, preferred_element_type=F32)
            part = part.reshape(GROUP, KB, KB)
            if start:
                hacc[i0:i0 + GROUP] = part
            else:
                hacc[i0:i0 + GROUP] += part
            if last and i0 < NI:
                for i in range(i0, i0 + GROUP, 2):
                    fold(i)

    def row_col():
        return (lax.broadcasted_iota(jnp.int32, (KB, KB), 0), lax.broadcasted_iota(jnp.int32, (KB, KB), 1))

    def diagonal(square):
        row, col = row_col()
        kept = jnp.where(row == col, square, 0.0)
        return jnp.sum(kept, axis=0, keepdims=True), jnp.sum(kept, axis=1, keepdims=True)

    def inverse_root(d):
        root = jnp.sqrt(d)
        return jnp.where(root > TINY, 1.0 / jnp.maximum(root, TINY), 0.0)

    def fold(i):
        row, col = row_col()
        upper, lower = hacc[i], hacc[i + 1]
        upper_row, upper_col = diagonal(upper)
        lower_row, lower_col = diagonal(lower)
        square = jnp.where(row <= col, upper, lower)
        by_col = jnp.where(row <= col, inverse_root(upper_col), inverse_root(lower_col))
        by_row = jnp.where(row <= col, inverse_root(upper_row), inverse_root(lower_row))
        coded = jnp.round(square * by_col * by_row * STEPS)
        coded = jnp.minimum(jnp.maximum(coded, -32767.0), 32767.0)
        hsend[i // 2] = coded.astype(jnp.int32).astype(jnp.int16)
        first = lax.broadcasted_iota(jnp.int32, (8, KB), 0) == 0
        dsend[i // 2] = jnp.where(first, upper_row, lower_row)
        send(("h", i), hsend.at[i // 2], hin.at[i // 2], partner)
        send(("d", i), dsend.at[i // 2], din.at[i // 2], partner)

    def own_systems():
        prior = PRIOR * gall[:, 0].reshape(KB, KB)
        for i in range(NI):
            h = hacc[NI + i]
            hown[i] = 0.5 * (h + h.T) + prior

    def join_systems():
        row, col = row_col()
        for i in range(0, NI, 2):
            arrived(("d", i), din.at[i // 2])
            upper_row, lower_row = din[i // 2, 0:1], din[i // 2, 1:2]
            upper_root, lower_root = jnp.sqrt(upper_row), jnp.sqrt(lower_row)
            as_col = lambda r: jnp.sum(jnp.where(row == col, r, 0.0), axis=1, keepdims=True)
            by_col = jnp.where(row <= col, as_col(upper_root), as_col(lower_root))
            by_row = jnp.where(row <= col, upper_root, lower_root)
            scale = by_col * by_row * (1.0 / STEPS)
            arrived(("h", i), hin.at[i // 2])
            square = hin[i // 2].astype(jnp.int32).astype(F32) * scale
            turned = square.T
            first = jnp.where(row < col, square, jnp.where(row == col, upper_row, turned))
            second = jnp.where(row > col, square, jnp.where(row == col, lower_row, turned))
            system_ref[pl.ds(i, KB, stride=NI), :] = hown[i] + first
            system_ref[pl.ds(i + 1, KB, stride=NI), :] = hown[i + 1] + second

    def drain():
        for copy in sent:
            copy.wait_send()
        sent.clear()

    def grad_part(q):
        left = zbufs[q][z].reshape(CU, KB)
        right = rights[q][...].reshape(CU, KB)
        pred = lax.dot_general(item[:, :KB], left, BOTH_LAST, preferred_element_type=F32)
        pred += lax.dot_general(item[:, KB:], right, BOTH_LAST, preferred_element_type=F32)
        w = wt_own[:, :, pl.ds(q * CU, CU)].reshape(TILE, CU).astype(F32)
        t = tt_own[:, :, pl.ds(q * CU, CU)].reshape(TILE, CU).astype(F32)
        resid = (w * (pred - t)).astype(BF16)
        part = jnp.dot(resid, left, preferred_element_type=F32).reshape(16, NI, KB)
        if q == 0:
            gsend[...] = part
        else:
            gsend[...] += part

    def grad_start():
        send_all("gr", [(gsend.at[grp_at[k]], gin.at[me_g], grp_peer[k]) for k in range(1, 16)])
        gin[me_g] = gsend[me_g]

    def rhs_start():
        itemf[...] = item[...].astype(F32)
        mine = itemf[pl.ds(me_g * NI, NI), :]
        mine_ref[...] = mine[:, :KB]
        exact = lax.Precision.HIGHEST
        rhs_ref[...] = PRIOR * (
            lax.dot_general(mine[:, :KB], gall[:, 0].reshape(KB, KB), BOTH_LAST,
                            precision=exact, preferred_element_type=F32)
            + lax.dot_general(mine[:, KB:], gall[:, 1].reshape(KB, KB), BOTH_LAST,
                              precision=exact, preferred_element_type=F32))

    def grad_last():
        all_arrived("gr", gin.at[pl.ds(0, 15)])
        rhs_ref[...] += jnp.sum(gin[...], axis=0)

    def target_ready():
        fetched("target")
        transposed(target, tt_own)
        fetched("item")

    def send_requests():
        fetched("tile")
        for k in range(1, 4):
            send(("rq", k), reqs.at[x], reqs.at[x], x_peer[k])

    def requests_arrived():
        for k in range(1, 4):
            arrived(("rq", k), reqs.at[x_at[4 - k]])

    send_requests()
    send_chunk(0)
    send_chunk(1)
    send_chunk(2)
    send_weights()
    gram_start()
    target_ready()
    forward_chunk(0)
    send_chunk(3)
    requests_arrived()
    finish_pool(0)
    x_pack(0)
    forward_chunk(1)
    send_chunk(4)
    weights_arrived()
    finish_pool(1)
    x_pack(1)
    forward_chunk(2)
    send_chunk(5)
    gram_second()
    finish_pool(2)
    x_pack(2)
    forward_chunk(3)
    send_chunk(6)
    x_final(0)
    z_start(0)
    x_final(1)
    z_start(1)
    finish_pool(3)
    x_pack(3)
    forward_chunk(4)
    send_chunk(7)
    z_hop(0, 1)
    hess_piece(0, (z_at[7], z_at[1]), start=True)
    finish_pool(4)
    x_pack(4)
    forward_chunk(5)
    x_final(2)
    z_start(2)
    z_hop(1, 1)
    hess_piece(1, (z_at[7], z_at[1]))
    z_hop(0, 2)
    hess_piece(0, (z_at[6], z_at[2]))
    finish_pool(5)
    x_pack(5)
    forward_chunk(6)
    x_final(3)
    z_start(3)
    z_hop(2, 1)
    hess_piece(2, (z_at[7], z_at[1]))
    gram_third()
    finish_pool(6)
    x_pack(6)
    forward_chunk(7)
    x_final(4)
    z_hop(1, 2)
    grad_part(0)
    z_hop(0, 3)
    hess_piece(1, (z_at[6], z_at[2]))
    hess_piece(0, (z_at[5], z_at[3]))
    z_hop(3, 1)
    finish_pool(7)
    x_pack(7)
    hess_piece(3, (z_at[7], z_at[1]))
    x_final(5)
    z_hop(2, 2)
    grad_part(1)
    hess_piece(2, (z_at[6], z_at[2]))
    z_hop(1, 3)
    hess_piece(1, (z_at[5], z_at[3]))
    x_final(6)
    z_hop(0, 4)
    grad_part(2)
    hess_piece(0, (z, z_at[4]))
    z_hop(3, 2)
    hess_piece(3, (z_at[6], z_at[2]))
    x_final(7)
    z_hop(2, 3)
    grad_part(3)
    grad_start()
    z_hop(1, 4)
    hess_piece(2, (z_at[5], z_at[3]))
    z_hop(3, 3)
    gram_last()
    rhs_start()
    hess_piece(1, (z, z_at[4]))
    z_hop(2, 4)
    hess_piece(3, (z_at[5], z_at[3]))
    hess_piece(2, (z, z_at[4]))
    z_hop(3, 4)
    hess_piece(3, (z, z_at[4]), last=True)
    own_systems()
    drain()
    grad_last()
    join_systems()
    for copy in sent:
        copy.wait_send()
    assert len(slots) <= NSEM, len(slots)
    solve(system_ref, rhs_ref, mine_ref, out_ref, dinv_ref)


NSEM = 180


def normal_equations(user_factors, item_factors, tile_user, tile_weight, tile_target):
    vm = pltpu.VMEM
    chunk = (NT, ROWS // 2, KB)
    both = (2,) + chunk
    return pl.pallas_call(
        gather_kernel,
        out_shape=jax.ShapeDtypeStruct((NI, KB), F32),
        in_specs=[pl.BlockSpec(memory_space=pl.ANY)] * 5,
        out_specs=pl.BlockSpec(memory_space=pltpu.VMEM),
        scratch_shapes=[
            [vm((4, OWN, ROWS, KB), BF16)] * NCH,
            [vm(chunk, BF16)] * NCH,
            [vm(chunk, BF16)] * NCH,
            [vm(both, BF16)] * NCH,
            [vm(both, BF16)] * NCH,
            [vm(chunk, BF16)] * NCH,
            [vm(chunk, BF16)] * NCH,
            [vm(both, BF16)] * NCH,
            [vm(both, BF16)] * NCH,
            [vm((NT, ROWS, KB), BF16)] * NQ,
            [vm((NZ, NT, ROWS, KB), BF16)] * NQ,
            pltpu.SMEM((4, 1, NT), jnp.int32),
            vm((TILE, K), BF16),
            vm((TILE, K), F32),
            vm((NT, TILE, TILE), BF16),
            vm((NT, TILE, TILE), BF16),
            vm((NZ, 16, NT * TILE), BF16),
            vm((NZ, 16, NT * TILE), BF16),
            vm((NZ, 16, NT * TILE), BF16),
            vm((16, KB, KB), F32),
            vm((NI // 2, KB, KB), jnp.int16),
            vm((NI // 2, KB, KB), jnp.int16),
            vm((NI // 2, 8, KB), F32),
            vm((NI // 2, 8, KB), F32),
            vm((NI, KB, KB), F32),
            vm((16, NI, KB), F32),
            vm((16, NI, KB), F32),
            vm((16, 2, 8, KB), F32),
            vm((16, 2, 8, KB), F32),
            vm((2, 8, KB), F32),
            vm((16, 2, 8, KB), F32),
            vm((2, 8, KB), F32),
            vm((16, 2, 8, KB), F32),
            vm((KB * NI, KB), F32),
            vm((NI, KB), F32),
            vm((NI, KB), F32),
            vm((KB // PANEL, PANEL * (PANEL + 1) // 2, NI, KB), F32),
            pltpu.SemaphoreType.DMA((NCH + 4,)),
            pltpu.SemaphoreType.DMA((NSEM,)),
            pltpu.SemaphoreType.DMA((NSEM,)),
        ],
        compiler_params=pltpu.CompilerParams(
            collective_id=0, has_side_effects=True, vmem_limit_bytes=60 * 1024 * 1024),
        name="normal_equations",
    )(user_factors, tile_user, item_factors, tile_weight, tile_target)


def lane_bcast(v, lane):
    return jnp.broadcast_to(v[:, lane:lane+1], v.shape)

def tree(xs):
    while len(xs) > 1:
        xs = [xs[i] + xs[i+1] if i+1 < len(xs) else xs[i] for i in range(0, len(xs), 2)]
    return xs[0]

def split(v):
    h = v.astype(BF16)
    rest = v - h.astype(F32)
    m = rest.astype(BF16)
    return h, m, (rest - m.astype(F32)).astype(BF16)


def sweep_inverse(d, n):
    g = lambda i, j: d[(i, j) if i <= j else (j, i)]
    for k in range(n):
        inv = 1.0 / g(k, k)
        scaled = {i: g(i, k) * inv for i in range(n) if i != k}
        new = {}
        for i in range(n):
            for j in range(i, n):
                if i == k and j == k:
                    new[(i, j)] = -inv
                elif i == k:
                    new[(i, j)] = scaled[j]
                elif j == k:
                    new[(i, j)] = scaled[i]
                else:
                    new[(i, j)] = d[(i, j)] - scaled[i] * g(j, k)
        d = new
        g = lambda i, j, d=d: d[(i, j) if i <= j else (j, i)]
    return {ij: -v for ij, v in d.items()}

def solve(a_ref, rhs_ref, mine_ref, out_ref, dinv_ref):
    lane = lax.broadcasted_iota(jnp.int32, (NI, KB), 1)
    b = rhs_ref[...]
    pairs = [(i, j) for i in range(PANEL) for j in range(i, PANEL)]
    for p in range(KB // PANEL):
        k0 = p * PANEL
        rows = [a_ref[pl.ds((k0 + j) * NI, NI), :] for j in range(PANEL)]
        dinv = sweep_inverse({(i, j): lane_bcast(rows[i], k0 + j) for i, j in pairs}, PANEL)
        for n, ij in enumerate(pairs):
            dinv_ref[p, n] = dinv[ij]
        if p + 1 == KB // PANEL:
            break
        kept = [jnp.where(lane >= k0 + PANEL, r, 0.0) for r in rows]
        ws = [tree([dinv[(min(i, j), max(i, j))] * kept[j] for j in range(PANEL)]) for i in range(PANEL)]
        b = b - tree([lane_bcast(b, k0 + j) * ws[j] for j in range(PANEL)])
        first = (k0 + PANEL) * NI
        rest = a_ref[first:, :]
        count = KB * NI - first
        at = lax.broadcasted_iota(jnp.int32, (count, KB), 1)
        spread = jnp.take_along_axis(
            rest, k0 + jnp.bitwise_and(jnp.right_shift(at, 3), PANEL - 1), axis=1, mode="promise_in_bounds")
        item = jnp.bitwise_and(lax.broadcasted_iota(jnp.int32, (count, KB), 0), NI - 1)
        spread = jnp.where(jnp.bitwise_and(at, NI - 1) == item, spread, 0.0)
        h, m, l = split(spread)
        wh, wm, wl = split(jnp.concatenate(ws, axis=0))
        far = jnp.where(at < NI * PANEL, h.astype(F32), l.astype(F32)).astype(BF16)
        a_ref[first:, :] = rest - jnp.dot(
            jnp.concatenate([h, m, far], axis=1), jnp.concatenate([wh, wm, wh, wm, wl, wh], axis=0),
            preferred_element_type=F32)
    x = jnp.zeros((NI, KB), F32)
    for p in range(KB // PANEL - 1, -1, -1):
        k0 = p * PANEL
        bs = [lane_bcast(b, k0 + j) for j in range(PANEL)]
        dinv = {ij: dinv_ref[p, n] for n, ij in enumerate(pairs)}
        xs = [tree([dinv[(min(i, j), max(i, j))] * bs[j] for j in range(PANEL)]) for i in range(PANEL)]
        for j in range(PANEL):
            x = jnp.where(lane == k0 + j, xs[j], x)
        if p:
            b = b - tree([xs[j] * jnp.where(lane < k0, a_ref[pl.ds((k0 + j) * NI, NI), :], 0.0) for j in range(PANEL)])
    out_ref[...] = mine_ref[...] - x


def local(user_factors, item_factors, tile_user, tile_weight, tile_target):
    return normal_equations(
        user_factors.reshape(OWN, TILE, K), item_factors, tile_user[0], tile_weight[0, 0], tile_target[0, 0])


def solution(mesh):
    return jax.shard_map(
        local,
        mesh=mesh,
        in_specs=(
            P("grp", "blk", None),
            P("blk", None),
            P("blk", "grp", None),
            P("blk", "grp", None, None, None),
            P("blk", "grp", None, None, None),
        ),
        out_specs=P(("blk", "grp"), None),
        check_vma=False,
    )
```

```python
import functools

import jax
import jax.numpy as jnp
from jax import lax
from jax.experimental import pallas as pl
from jax.experimental.pallas import tpu as pltpu
from jax.sharding import PartitionSpec as P

F32 = jnp.float32
BF16 = jnp.bfloat16
MESH = pl.DeviceIdType.MESH
K = 256
KB = 128
TILE = 128
NT = 8
PRIOR = 0.05
NI = 8
OWN = 16
ROWS = 32
NQ = TILE // ROWS
NCH = 2 * NQ
CU = NT * ROWS
NZ = 8
PANEL = 8
STEPS = 32000.0
TINY = 1e-18
BOTH_LAST = (((1,), (1,)), ((), ()))
BOTH_FIRST = (((0,), (0,)), ((), ()))


def gather_kernel(
    user_ref, tile_ref, item_ref, weight_ref, target_ref,
    out_ref,
    pools, far_a, far_b, out_p, out_m, in_a, in_b, in_p, in_m, rights, zbufs,
    reqs, item, itemf, weight, target, wt_own, tt_own, wz, hacc, hsend, hin, dsend, din, hown, gsend, gin,
    gpart, gin1, gone, gin2, gtwo, gall, system_ref, rhs_ref, mine_ref, dinv_ref, local_sem, send_sem, recv_sem,
):
    me_b, me_g = lax.axis_index("blk"), lax.axis_index("grp")
    y_lo, x, core = me_b // 8, lax.rem(me_b // 2, 4), lax.rem(me_b, 2)
    z, y_hi = me_g // 2, lax.rem(me_g, 2)
    own = y_lo * 2 + core
    across = (1 - y_lo) * 2 + core
    sibling = (me_b + 1 - 2 * core, me_g)
    y_peer = (lax.rem(me_b + 8, 16), me_g)
    x_at = [lax.rem(x + k, 4) for k in range(4)]
    x_peer = [(y_lo * 8 + x_at[k] * 2 + core, me_g) for k in range(4)]
    z_at = [lax.rem(z + k, NZ) for k in range(NZ)]
    z_peer = [(me_b, z_at[k] * 2 + y_hi) for k in range(NZ)]
    blk_at = [lax.rem(me_b + k, 16) for k in range(16)]
    grp_at = [lax.rem(me_g + k, 16) for k in range(16)]
    blk_peer = [(blk_at[k], me_g) for k in range(16)]
    grp_peer = [(me_b, grp_at[k]) for k in range(16)]
    partner = (me_b, me_g + 1 - 2 * y_hi)

    slots, sent = {}, []

    def slot(name):
        return slots.setdefault(name, len(slots))

    def send(name, src, dst, device):
        k = slot(name)
        copy = pltpu.make_async_remote_copy(
            src_ref=src, dst_ref=dst, send_sem=send_sem.at[k], recv_sem=recv_sem.at[k],
            device_id=device, device_id_type=MESH)
        copy.start()
        sent.append(copy)

    def arrived(name, dst):
        k = slot(name)
        pltpu.make_async_remote_copy(
            src_ref=dst, dst_ref=dst, send_sem=send_sem.at[k], recv_sem=recv_sem.at[k],
            device_id=sibling, device_id_type=MESH).wait_recv()

    def send_all(name, pairs):
        k = slot(name)
        for src, dst, device in pairs:
            copy = pltpu.make_async_remote_copy(
                src_ref=src, dst_ref=dst, send_sem=send_sem.at[k], recv_sem=recv_sem.at[k],
                device_id=device, device_id_type=MESH)
            copy.start()

    def all_of(name, whole):
        k = slot(name)
        return pltpu.make_async_remote_copy(
            src_ref=whole, dst_ref=whole, send_sem=send_sem.at[k], recv_sem=recv_sem.at[k],
            device_id=sibling, device_id_type=MESH)

    def all_arrived(name, whole):
        copy = all_of(name, whole)
        copy.wait_recv()
        sent.append(copy)

    locals_ = {}

    def fetch(name, src, dst):
        copy = pltpu.make_async_copy(src, dst, local_sem.at[len(locals_)])
        copy.start()
        locals_[name] = copy

    fetch("tile", tile_ref, reqs.at[x])
    for c in range(NCH):
        rows, cols = (c % NQ) * ROWS, (c // NQ) * KB
        fetch(("pool", c), user_ref.at[:, pl.ds(rows, ROWS), pl.ds(cols, KB)], pools[c].at[own])
    fetch("weight", weight_ref, weight)
    fetch("target", target_ref, target)
    fetch("item", item_ref, item)

    barrier = pltpu.get_barrier_semaphore()
    for k in range(1, 16):
        pl.semaphore_signal(barrier, inc=1, device_id=blk_peer[k], device_id_type=MESH)
        pl.semaphore_signal(barrier, inc=1, device_id=grp_peer[k], device_id_type=MESH)

    def fetched(name):
        if name in locals_:
            locals_.pop(name).wait()

    pl.semaphore_wait(barrier, 30)

    def send_chunk(c):
        fetched(("pool", c))
        send(("y", c), pools[c].at[own], pools[c].at[own], y_peer)
        send(("s", c), pools[c].at[own], pools[c].at[own], sibling)

    def forward_chunk(c):
        arrived(("y", c), pools[c].at[across])
        send(("f", c), pools[c].at[across], pools[c].at[across], sibling)

    def finish_pool(c):
        other = y_lo * 2 + 1 - core
        diagonal = (1 - y_lo) * 2 + 1 - core
        arrived(("s", c), pools[c].at[other])
        arrived(("f", c), pools[c].at[diagonal])

    def wanted(k, j):
        return reqs[x_at[k], 0, j]

    def column(t):
        return jnp.bitwise_and(jnp.right_shift(t, 5), 3)

    def pick(c, t):
        owner = jnp.right_shift(t, 7) * 2 + jnp.bitwise_and(jnp.right_shift(t, 4), 1)
        return pools[c][owner, jnp.bitwise_and(t, 15)]

    half = ROWS // 2

    def x_pack(c):
        for j in range(NT):
            v = pick(c, wanted(2, j))
            far_a[c][j] = v[:half]
            far_b[c][j] = v[half:]
        send(("xa", c), far_a[c], in_a[c], x_peer[2])
        send(("xb", c), far_b[c], in_b[c], x_peer[2])
        for j in range(NT):
            v = pick(c, wanted(1, j))
            out_p[c][0, j] = v[:half]
            out_p[c][1, j] = v[half:]
            v = pick(c, wanted(3, j))
            out_m[c][0, j] = v[:half]
            out_m[c][1, j] = v[half:]
        send(("p0", c), out_p[c], in_m[c], x_peer[1])
        send(("m0", c), out_m[c], in_p[c], x_peer[3])

    def x_final(c):
        arrived(("p0", c), in_m[c])
        arrived(("m0", c), in_p[c])
        arrived(("xa", c), in_a[c])
        arrived(("xb", c), in_b[c])
        for j in range(NT):
            t = wanted(0, j)
            away = jnp.bitwise_and(column(t) - x + 4, 3)
            mine = pick(c, t)
            parts = []
            for p, far in ((0, in_a[c][j]), (1, in_b[c][j])):
                near = jnp.where(away == 1, in_p[c][p, j], in_m[c][p, j])
                parts.append(jnp.where(away == 0, mine[p * half:(p + 1) * half], jnp.where(away == 2, far, near)))
            put(c, j, *parts)

    def put(c, j, first, second):
        if c < NQ:
            zbufs[c][z, j, :half] = first
            zbufs[c][z, j, half:] = second
        else:
            rights[c - NQ][j, :half] = first
            rights[c - NQ][j, half:] = second

    def slots_of(q, source, part):
        return zbufs[q].at[source, pl.ds(part * (NT // 2), NT // 2)]

    def z_start(q):
        for first in (0, 1):
            for side, part, peer in (("zr", first, z_peer[1]), ("zl", 1 - first, z_peer[7])):
                mine = slots_of(q, z, part)
                send((side, q, 1, part), mine, mine, peer)

    def z_hop(q, h):
        for first in (0, 1) if h < 4 else (0,):
            for side, part, source, peer in (
                ("zr", first, z_at[NZ - h], z_peer[1]), ("zl", 1 - first, z_at[h], z_peer[7])):
                here = slots_of(q, source, part)
                arrived((side, q, h, part), here)
                if h < 3 or (h == 3 and first == 0):
                    send((side, q, h + 1, part), here, here, peer)

    def transposed(ref, out):
        span = TILE // ROWS
        for q in range(NQ):
            for p in range(NT // span):
                block = ref[p * span:(p + 1) * span, q * ROWS:(q + 1) * ROWS, :].reshape(TILE, TILE)
                out[:, :, pl.ds((q * (NT // span) + p) * TILE, TILE)] = block.T.reshape(NZ, 16, TILE)

    def send_weights():
        fetched("weight")
        transposed(weight, wt_own)
        send_all("w", [(wt_own.at[z_at[k]], wz.at[z], z_peer[k]) for k in range(1, NZ)])
        wz[z] = wt_own[z]

    def weights_arrived():
        all_arrived("w", wz.at[pl.ds(0, NZ - 1)])

    def gram_start():
        for c in range(NCH):
            fetched(("pool", c))
        left = jnp.zeros((KB, KB), F32)
        right = jnp.zeros((KB, KB), F32)
        for q in range(NQ):
            a = pools[q][own].reshape(OWN * ROWS, KB)
            b = pools[NQ + q][own].reshape(OWN * ROWS, KB)
            left += lax.dot_general(a, a, BOTH_FIRST, preferred_element_type=F32)
            right += lax.dot_general(a, b, BOTH_FIRST, preferred_element_type=F32)
        gpart[:, 0] = left.reshape(16, 8, KB)
        gpart[:, 1] = right.reshape(16, 8, KB)
        send_all("g1", [(gpart.at[blk_at[k]], gin1.at[me_b], blk_peer[k]) for k in range(1, 16)])
        gin1[me_b] = gpart[me_b]

    def gram_second():
        all_arrived("g1", gin1.at[pl.ds(0, 15)])
        gone[...] = jnp.sum(gin1[...], axis=0)
        send_all("g2", [(gone, gin2.at[me_g], grp_peer[k]) for k in range(1, 16)])
        gin2[me_g] = gone[...]

    def gram_third():
        all_arrived("g2", gin2.at[pl.ds(0, 15)])
        gtwo[...] = jnp.sum(gin2[...], axis=0)
        send_all("g3", [(gtwo, gall.at[me_b], blk_peer[k]) for k in range(1, 16)])
        gall[me_b] = gtwo[...]

    def gram_last():
        all_arrived("g3", gall.at[pl.ds(0, 15)])

    def hess_piece(q, sources, start=False, last=False):
        users = [zbufs[q][s].reshape(CU, KB) for s in sources]
        users_t = jnp.concatenate(
            [u[p * KB:(p + 1) * KB].T for u in users for p in range(CU // KB)], axis=1)
        width = CU * len(sources)
        users_t = users_t.reshape(KB // 16, 16, width)
        users = jnp.concatenate(users, axis=0)
        scale = jnp.concatenate([wz[s, :, pl.ds(q * CU, CU)].astype(F32) for s in sources], axis=1)
        theirs = jnp.where(y_hi == 0, scale[8:], scale[:8])
        ours = jnp.where(y_hi == 0, scale[:8], scale[8:])
        scale = jnp.concatenate([theirs, ours], axis=0)
        group = 4 if last else 8
        for i0 in range(0, 16, group):
            lhs = []
            for i in range(i0, i0 + group):
                row = jnp.broadcast_to(scale[i:i + 1], (16, width)).astype(BF16)
                lhs.append((row[None] * users_t).reshape(KB, width))
            part = jnp.dot(jnp.concatenate(lhs, axis=0), users, preferred_element_type=F32)
            part = part.reshape(group, KB, KB)
            if start:
                hacc[i0:i0 + group] = part
            else:
                hacc[i0:i0 + group] += part
            if last and i0 < NI:
                for i in range(i0, i0 + group, 2):
                    fold(i)

    def row_col():
        return (lax.broadcasted_iota(jnp.int32, (KB, KB), 0), lax.broadcasted_iota(jnp.int32, (KB, KB), 1))

    def diagonal(square):
        row, col = row_col()
        kept = jnp.where(row == col, square, 0.0)
        return jnp.sum(kept, axis=0, keepdims=True), jnp.sum(kept, axis=1, keepdims=True)

    def inverse_root(d):
        root = jnp.sqrt(d)
        return jnp.where(root > TINY, 1.0 / jnp.maximum(root, TINY), 0.0)

    def fold(i):
        row, col = row_col()
        upper, lower = hacc[i], hacc[i + 1]
        upper_row, upper_col = diagonal(upper)
        lower_row, lower_col = diagonal(lower)
        square = jnp.where(row <= col, upper, lower)
        by_col = jnp.where(row <= col, inverse_root(upper_col), inverse_root(lower_col))
        by_row = jnp.where(row <= col, inverse_root(upper_row), inverse_root(lower_row))
        coded = jnp.round(square * by_col * by_row * STEPS)
        coded = jnp.minimum(jnp.maximum(coded, -32767.0), 32767.0)
        hsend[i // 2] = coded.astype(jnp.int32).astype(jnp.int16)
        first = lax.broadcasted_iota(jnp.int32, (8, KB), 0) == 0
        dsend[i // 2] = jnp.where(first, upper_row, lower_row)
        send(("h", i), hsend.at[i // 2], hin.at[i // 2], partner)
        send(("d", i), dsend.at[i // 2], din.at[i // 2], partner)

    def own_systems():
        prior = PRIOR * gall[:, 0].reshape(KB, KB)
        for i in range(NI):
            h = hacc[NI + i]
            hown[i] = 0.5 * (h + h.T) + prior

    def join_systems():
        row, col = row_col()
        for i in range(0, NI, 2):
            arrived(("d", i), din.at[i // 2])
            upper_row, lower_row = din[i // 2, 0:1], din[i // 2, 1:2]
            upper_root, lower_root = jnp.sqrt(upper_row), jnp.sqrt(lower_row)
            as_col = lambda r: jnp.sum(jnp.where(row == col, r, 0.0), axis=1, keepdims=True)
            by_col = jnp.where(row <= col, as_col(upper_root), as_col(lower_root))
            by_row = jnp.where(row <= col, upper_root, lower_root)
            scale = by_col * by_row * (1.0 / STEPS)
            arrived(("h", i), hin.at[i // 2])
            square = hin[i // 2].astype(jnp.int32).astype(F32) * scale
            turned = square.T
            first = jnp.where(row < col, square, jnp.where(row == col, upper_row, turned))
            second = jnp.where(row > col, square, jnp.where(row == col, lower_row, turned))
            system_ref[pl.ds(i, KB, stride=NI), :] = hown[i] + first
            system_ref[pl.ds(i + 1, KB, stride=NI), :] = hown[i + 1] + second

    def drain():
        for copy in sent:
            copy.wait_send()
        sent.clear()

    def grad_part(q):
        left = zbufs[q][z].reshape(CU, KB)
        right = rights[q][...].reshape(CU, KB)
        pred = lax.dot_general(item[:, :KB], left, BOTH_LAST, preferred_element_type=F32)
        pred += lax.dot_general(item[:, KB:], right, BOTH_LAST, preferred_element_type=F32)
        w = wt_own[:, :, pl.ds(q * CU, CU)].reshape(TILE, CU).astype(F32)
        t = tt_own[:, :, pl.ds(q * CU, CU)].reshape(TILE, CU).astype(F32)
        resid = (w * (pred - t)).astype(BF16)
        part = jnp.dot(resid, left, preferred_element_type=F32).reshape(16, NI, KB)
        if q == 0:
            gsend[...] = part
        else:
            gsend[...] += part

    def grad_start():
        send_all("gr", [(gsend.at[grp_at[k]], gin.at[me_g], grp_peer[k]) for k in range(1, 16)])
        gin[me_g] = gsend[me_g]

    def rhs_start():
        itemf[...] = item[...].astype(F32)
        mine = itemf[pl.ds(me_g * NI, NI), :]
        mine_ref[...] = mine[:, :KB]
        exact = lax.Precision.HIGHEST
        rhs_ref[...] = PRIOR * (
            lax.dot_general(mine[:, :KB], gall[:, 0].reshape(KB, KB), BOTH_LAST,
                            precision=exact, preferred_element_type=F32)
            + lax.dot_general(mine[:, KB:], gall[:, 1].reshape(KB, KB), BOTH_LAST,
                              precision=exact, preferred_element_type=F32))

    def grad_last():
        all_arrived("gr", gin.at[pl.ds(0, 15)])
        rhs_ref[...] += jnp.sum(gin[...], axis=0)

    def target_ready():
        fetched("target")
        transposed(target, tt_own)
        fetched("item")

    def send_requests():
        fetched("tile")
        for k in range(1, 4):
            send(("rq", k), reqs.at[x], reqs.at[x], x_peer[k])

    def requests_arrived():
        for k in range(1, 4):
            arrived(("rq", k), reqs.at[x_at[4 - k]])

    send_requests()
    send_chunk(0)
    send_chunk(1)
    send_chunk(2)
    send_weights()
    gram_start()
    target_ready()
    forward_chunk(0)
    send_chunk(3)
    requests_arrived()
    finish_pool(0)
    x_pack(0)
    forward_chunk(1)
    send_chunk(4)
    weights_arrived()
    finish_pool(1)
    x_pack(1)
    forward_chunk(2)
    send_chunk(5)
    gram_second()
    finish_pool(2)
    x_pack(2)
    forward_chunk(3)
    send_chunk(6)
    x_final(0)
    z_start(0)
    x_final(1)
    z_start(1)
    finish_pool(3)
    x_pack(3)
    forward_chunk(4)
    send_chunk(7)
    z_hop(0, 1)
    hess_piece(0, (z_at[7], z_at[1]), start=True)
    finish_pool(4)
    x_pack(4)
    forward_chunk(5)
    x_final(2)
    z_start(2)
    z_hop(1, 1)
    hess_piece(1, (z_at[7], z_at[1]))
    z_hop(0, 2)
    hess_piece(0, (z_at[6], z_at[2]))
    finish_pool(5)
    x_pack(5)
    forward_chunk(6)
    x_final(3)
    z_start(3)
    z_hop(2, 1)
    hess_piece(2, (z_at[7], z_at[1]))
    gram_third()
    finish_pool(6)
    x_pack(6)
    forward_chunk(7)
    x_final(4)
    z_hop(1, 2)
    grad_part(0)
    z_hop(0, 3)
    hess_piece(1, (z_at[6], z_at[2]))
    hess_piece(0, (z_at[5], z_at[3]))
    z_hop(3, 1)
    finish_pool(7)
    x_pack(7)
    hess_piece(3, (z_at[7], z_at[1]))
    x_final(5)
    z_hop(2, 2)
    grad_part(1)
    hess_piece(2, (z_at[6], z_at[2]))
    z_hop(1, 3)
    hess_piece(1, (z_at[5], z_at[3]))
    x_final(6)
    z_hop(0, 4)
    grad_part(2)
    hess_piece(0, (z, z_at[4]))
    z_hop(3, 2)
    hess_piece(3, (z_at[6], z_at[2]))
    x_final(7)
    z_hop(2, 3)
    grad_part(3)
    grad_start()
    z_hop(1, 4)
    hess_piece(2, (z_at[5], z_at[3]))
    z_hop(3, 3)
    gram_last()
    rhs_start()
    hess_piece(1, (z, z_at[4]))
    z_hop(2, 4)
    hess_piece(3, (z_at[5], z_at[3]))
    hess_piece(2, (z, z_at[4]))
    z_hop(3, 4)
    hess_piece(3, (z, z_at[4]), last=True)
    own_systems()
    drain()
    grad_last()
    join_systems()
    for copy in sent:
        copy.wait_send()
    assert len(slots) <= NSEM, len(slots)
    solve(system_ref, rhs_ref, mine_ref, out_ref, dinv_ref)


NSEM = 180


def normal_equations(user_factors, item_factors, tile_user, tile_weight, tile_target):
    vm = pltpu.VMEM
    chunk = (NT, ROWS // 2, KB)
    both = (2,) + chunk
    return pl.pallas_call(
        gather_kernel,
        out_shape=jax.ShapeDtypeStruct((NI, KB), F32),
        in_specs=[pl.BlockSpec(memory_space=pl.ANY)] * 5,
        out_specs=pl.BlockSpec(memory_space=pltpu.VMEM),
        scratch_shapes=[
            [vm((4, OWN, ROWS, KB), BF16)] * NCH,
            [vm(chunk, BF16)] * NCH,
            [vm(chunk, BF16)] * NCH,
            [vm(both, BF16)] * NCH,
            [vm(both, BF16)] * NCH,
            [vm(chunk, BF16)] * NCH,
            [vm(chunk, BF16)] * NCH,
            [vm(both, BF16)] * NCH,
            [vm(both, BF16)] * NCH,
            [vm((NT, ROWS, KB), BF16)] * NQ,
            [vm((NZ, NT, ROWS, KB), BF16)] * NQ,
            pltpu.SMEM((4, 1, NT), jnp.int32),
            vm((TILE, K), BF16),
            vm((TILE, K), F32),
            vm((NT, TILE, TILE), BF16),
            vm((NT, TILE, TILE), BF16),
            vm((NZ, 16, NT * TILE), BF16),
            vm((NZ, 16, NT * TILE), BF16),
            vm((NZ, 16, NT * TILE), BF16),
            vm((16, KB, KB), F32),
            vm((NI // 2, KB, KB), jnp.int16),
            vm((NI // 2, KB, KB), jnp.int16),
            vm((NI // 2, 8, KB), F32),
            vm((NI // 2, 8, KB), F32),
            vm((NI, KB, KB), F32),
            vm((16, NI, KB), F32),
            vm((16, NI, KB), F32),
            vm((16, 2, 8, KB), F32),
            vm((16, 2, 8, KB), F32),
            vm((2, 8, KB), F32),
            vm((16, 2, 8, KB), F32),
            vm((2, 8, KB), F32),
            vm((16, 2, 8, KB), F32),
            vm((KB * NI, KB), F32),
            vm((NI, KB), F32),
            vm((NI, KB), F32),
            vm((KB // PANEL, PANEL * (PANEL + 1) // 2, NI, KB), F32),
            pltpu.SemaphoreType.DMA((NCH + 4,)),
            pltpu.SemaphoreType.DMA((NSEM,)),
            pltpu.SemaphoreType.DMA((NSEM,)),
        ],
        compiler_params=pltpu.CompilerParams(
            collective_id=0, has_side_effects=True, vmem_limit_bytes=60 * 1024 * 1024),
        name="normal_equations",
    )(user_factors, tile_user, item_factors, tile_weight, tile_target)


def lane_bcast(v, lane):
    return jnp.broadcast_to(v[:, lane:lane+1], v.shape)

def tree(xs):
    while len(xs) > 1:
        xs = [xs[i] + xs[i+1] if i+1 < len(xs) else xs[i] for i in range(0, len(xs), 2)]
    return xs[0]

def split(v):
    h = v.astype(BF16)
    rest = v - h.astype(F32)
    m = rest.astype(BF16)
    return h, m, (rest - m.astype(F32)).astype(BF16)


def sweep_inverse(d, n):
    g = lambda i, j: d[(i, j) if i <= j else (j, i)]
    for k in range(n):
        inv = 1.0 / g(k, k)
        scaled = {i: g(i, k) * inv for i in range(n) if i != k}
        new = {}
        for i in range(n):
            for j in range(i, n):
                if i == k and j == k:
                    new[(i, j)] = -inv
                elif i == k:
                    new[(i, j)] = scaled[j]
                elif j == k:
                    new[(i, j)] = scaled[i]
                else:
                    new[(i, j)] = d[(i, j)] - scaled[i] * g(j, k)
        d = new
        g = lambda i, j, d=d: d[(i, j) if i <= j else (j, i)]
    return {ij: -v for ij, v in d.items()}

def solve(a_ref, rhs_ref, mine_ref, out_ref, dinv_ref):
    lane = lax.broadcasted_iota(jnp.int32, (NI, KB), 1)
    b = rhs_ref[...]
    pairs = [(i, j) for i in range(PANEL) for j in range(i, PANEL)]
    for p in range(KB // PANEL):
        k0 = p * PANEL
        rows = [a_ref[pl.ds((k0 + j) * NI, NI), :] for j in range(PANEL)]
        dinv = sweep_inverse({(i, j): lane_bcast(rows[i], k0 + j) for i, j in pairs}, PANEL)
        for n, ij in enumerate(pairs):
            dinv_ref[p, n] = dinv[ij]
        if p + 1 == KB // PANEL:
            break
        kept = [jnp.where(lane >= k0 + PANEL, r, 0.0) for r in rows]
        ws = [tree([dinv[(min(i, j), max(i, j))] * kept[j] for j in range(PANEL)]) for i in range(PANEL)]
        b = b - tree([lane_bcast(b, k0 + j) * ws[j] for j in range(PANEL)])
        first = (k0 + PANEL) * NI
        rest = a_ref[first:, :]
        count = KB * NI - first
        at = lax.broadcasted_iota(jnp.int32, (count, KB), 1)
        spread = jnp.take_along_axis(
            rest, k0 + jnp.bitwise_and(jnp.right_shift(at, 3), PANEL - 1), axis=1, mode="promise_in_bounds")
        item = jnp.bitwise_and(lax.broadcasted_iota(jnp.int32, (count, KB), 0), NI - 1)
        spread = jnp.where(jnp.bitwise_and(at, NI - 1) == item, spread, 0.0)
        h, m, l = split(spread)
        wh, wm, wl = split(jnp.concatenate(ws, axis=0))
        far = jnp.where(at < NI * PANEL, h.astype(F32), l.astype(F32)).astype(BF16)
        a_ref[first:, :] = rest - jnp.dot(
            jnp.concatenate([h, m, far], axis=1), jnp.concatenate([wh, wm, wh, wm, wl, wh], axis=0),
            preferred_element_type=F32)
    x = jnp.zeros((NI, KB), F32)
    for p in range(KB // PANEL - 1, -1, -1):
        k0 = p * PANEL
        bs = [lane_bcast(b, k0 + j) for j in range(PANEL)]
        dinv = {ij: dinv_ref[p, n] for n, ij in enumerate(pairs)}
        xs = [tree([dinv[(min(i, j), max(i, j))] * bs[j] for j in range(PANEL)]) for i in range(PANEL)]
        for j in range(PANEL):
            x = jnp.where(lane == k0 + j, xs[j], x)
        if p:
            b = b - tree([xs[j] * jnp.where(lane < k0, a_ref[pl.ds((k0 + j) * NI, NI), :], 0.0) for j in range(PANEL)])
    out_ref[...] = mine_ref[...] - x


def local(user_factors, item_factors, tile_user, tile_weight, tile_target):
    return normal_equations(
        user_factors.reshape(OWN, TILE, K), item_factors, tile_user[0], tile_weight[0, 0], tile_target[0, 0])


def solution(mesh):
    return jax.shard_map(
        local,
        mesh=mesh,
        in_specs=(
            P("grp", "blk", None),
            P("blk", None),
            P("blk", "grp", None),
            P("blk", "grp", None, None, None),
            P("blk", "grp", None, None, None),
        ),
        out_specs=P(("blk", "grp"), None),
        check_vma=False,
    )
```
